512 devices in a mesh: src: 128 (over z, x, core), tgt: 4 (over y).
Axes of the slice: x: 4, y: 4, z: 16, core: 2. Of those that a mesh axis runs over, the one named last changes fastest.
Arguments:
- source_cells: bfloat16 [65536, 256], P('src')
- target_cells: bfloat16 [8192, 256], P('tgt'), may hold values from -6 to 6
- source_mass: float32 [65536], P('src'), may hold values from 0.01 to 10
- target_mass: float32 [8192], P('tgt'), may hold values from 0.01 to 10
- pairs: int32 [128, 4, 32], P('src', 'tgt'), may hold values from 0 to 63, as said below
- counts: int32 [128, 4], P('src', 'tgt'), may hold values from 16 to 32, as said below
Outputs:
- row_potential: float32 [65536], P('src')
- col_potential: float32 [8192], P('tgt')
- mapped: float32 [65536, 256], P('src')
The draws below stay inside these ranges and needn't reach their ends.
Inputs may be any that keep to these rules, and one draw needn't show every extreme that they name: `pairs`: each entry is a source block times 16 plus a target block of that device; the entries of one device's list are distinct, and its first counts entries name every one of its 4 source blocks and every one of its 16 target blocks. `counts`: some device has 32 live entries.
All inputs are finite; a program needn't handle non-finite values.
Results may differ from the reference program's by a relative error of at most 0.0015.
Values sent between devices are 32-bit elements; how exact they have to be, the bound alone decides.
No kernel may reach another device: no remote copies, remote signals or barrier semaphores. Data moves between devices by JAX's collectives and lax.ppermute only.
A program may use at most 64 MiB of HBM per device.

```python
import math
import jax
import jax.numpy as jnp
from jax import lax

E = 256
BLOCK = 128
ITERS = 3
SB_DEV = 4
TB_DEV = 16
MAXB = 32
NS = 65536
NT = 8192
N_SRC = 128
N_TGT = 4


def draw_source_cells(key, part):
    key = jax.random.fold_in(key, 11)
    noise_key = jax.random.fold_in(key, 0)
    values = jax.random.normal(noise_key, (NS, E), jnp.float32)
    return values.astype(jnp.bfloat16)


def draw_pairs(key, part):
    key = jax.random.fold_in(key, 23)
    devices = N_SRC * N_TGT
    dense_count = SB_DEV * TB_DEV
    shift_key, order_key = jax.random.split(key, 2)
    shifts = jax.random.randint(shift_key, (devices,), 0, TB_DEV)
    order_keys = jax.random.split(order_key, devices)
    dense_ids = jnp.arange(dense_count)
    source_of = dense_ids // TB_DEV
    target_of = dense_ids % TB_DEV

    def device_list(shift, device_key):
        ranking = jax.random.permutation(device_key, dense_count)
        position = (target_of - shift) % TB_DEV
        covering = position % SB_DEV == source_of
        ordering = jnp.where(covering, ranking, ranking + dense_count)
        return jnp.argsort(ordering, stable=True)[:MAXB].astype(jnp.int32)
    return jax.vmap(device_list)(shifts, order_keys).reshape(N_SRC, N_TGT, MAXB)


def draw_counts(key, part):
    key = jax.random.fold_in(key, 37)
    devices = N_SRC * N_TGT
    extra_key, pick_key = jax.random.split(key, 2)
    extras = jax.random.randint(extra_key, (3, devices), 0, MAXB - TB_DEV + 1)
    counts = TB_DEV + jnp.min(extras, axis=0)
    chosen = jax.random.randint(pick_key, (), 0, devices)
    counts = jnp.where(jnp.arange(devices) == chosen, MAXB, counts)
    return counts.reshape(N_SRC, N_TGT).astype(jnp.int32)


def steps_of(stream_key, shape, cuts, least, high):
    factor_of, own = 1.0, jax.random.fold_in(stream_key, 6)
    for dim, shards_of in cuts:
        heights = jnp.exp(jax.random.uniform(jax.random.fold_in(own, dim), (shards_of,), jnp.float32, least / len(cuts), high / len(cuts)))
        factor_of = factor_of * jnp.repeat(heights, shape[dim] // shards_of).reshape([-1 if axis == dim else 1 for axis in range(len(shape))])
    return factor_of


def centred(key, shape, width, bound, cuts=(), dtype=jnp.bfloat16):
    result = width * jax.random.normal(key, shape, jnp.float32)
    if cuts:
        result = result * steps_of(key, shape, cuts, -0.22, 0.18)
    return jnp.clip(result, -bound, bound).astype(dtype)


def setup_inputs(seed: int = 0) -> dict:
    arg_keys = jax.random.split(jax.random.key(seed), 7)
    source_cells = draw_source_cells(jax.random.fold_in(arg_keys[6], 71), 0)
    target_cells = centred(arg_keys[1], (NT, E), 1.0, 6.0, ((0, 4),))
    source_mass = jnp.clip(jnp.exp(math.log(10.0) - 6.9077553 * jax.random.uniform(arg_keys[2], (NS,), jnp.float32) ** steps_of(arg_keys[2], (NS,), ((0, 128),), -0.2, 0.2)), 0.01, 10.0)
    target_mass = jnp.clip(jnp.exp(math.log(10.0) - 6.9077553 * jax.random.uniform(arg_keys[3], (NT,), jnp.float32) ** steps_of(arg_keys[3], (NT,), ((0, 4),), -0.2, 0.2)), 0.01, 10.0)
    pairs = draw_pairs(jax.random.fold_in(arg_keys[6], 71), 0)
    counts = draw_counts(jax.random.fold_in(arg_keys[6], 71), 0)
    return {"source_cells": source_cells, "target_cells": target_cells, "source_mass": source_mass, "target_mass": target_mass, "pairs": pairs, "counts": counts}


entropy = 0.02


def block_costs(embeddings, targets, slot_list, live_count):
    row_ids = slot_list // TB_DEV
    col_ids = slot_list % TB_DEV
    emb_width = embeddings.shape[1]
    src_blocks = embeddings.reshape(SB_DEV, BLOCK, emb_width)[row_ids].astype(jnp.float32)
    tgt_blocks = targets.reshape(TB_DEV, BLOCK, emb_width)[col_ids].astype(jnp.float32)
    crossed = jnp.einsum("bid,bjd->bij", src_blocks, tgt_blocks, precision=lax.Precision.HIGHEST)
    src_norm = jnp.sum(src_blocks * src_blocks, axis=-1)
    tgt_norm = jnp.sum(tgt_blocks * tgt_blocks, axis=-1)
    block_cost = (src_norm[:, :, None] + tgt_norm[:, None, :] - 2.0 * crossed) / E
    is_valid = jnp.arange(MAXB) < live_count
    return block_cost, row_ids, col_ids, is_valid, tgt_blocks


def group_max(scores, block_ids, group_count, reduce_axis):
    block_max = jnp.max(scores, axis=reduce_axis)
    onehot = block_ids[:, None] == jnp.arange(group_count)[None, :]
    return jnp.max(jnp.where(onehot[:, :, None], block_max[:, None, :], -jnp.inf), axis=0), onehot


def fold_blocks(scores, block_ids, group_count, reduce_axis):
    maxima, onehot = group_max(scores, block_ids, group_count, reduce_axis)
    shifted = jnp.expand_dims(maxima[block_ids], reduce_axis)
    partial_value = jnp.sum(jnp.exp(scores - shifted), axis=reduce_axis)
    sumexp = jnp.sum(jnp.where(onehot[:, :, None], partial_value[:, None, :], 0.0), axis=0)
    return maxima, sumexp


def combine(first, second):
    merged = jnp.maximum(first[0], second[0])
    return merged, first[1] * jnp.exp(first[0] - merged) + second[1] * jnp.exp(second[0] - merged)


def reference(source_cells, target_cells, source_mass, target_mass, pairs, counts):
    emb_width = source_cells.shape[1]
    sources = source_cells.reshape(N_SRC, SB_DEV * BLOCK, emb_width)
    targets = target_cells.reshape(N_TGT, TB_DEV * BLOCK, emb_width)
    source_log = jnp.log(source_mass).reshape(N_SRC, SB_DEV * BLOCK)
    target_log = jnp.log(target_mass).reshape(N_TGT, TB_DEV * BLOCK)
    col_pot = jnp.zeros((N_TGT, TB_DEV * BLOCK), jnp.float32)

    def row_update(col_pot):
        def per_source(inputs):
            embeddings, log_mass, slot_lists, live = inputs
            running = None
            for target in range(N_TGT):
                block_cost, row_ids, col_ids, is_valid, tgt_blocks = block_costs(embeddings, targets[target], slot_lists[target], live[target])
                potential_block = col_pot[target].reshape(TB_DEV, BLOCK)[col_ids]
                scores = jnp.where(is_valid[:, None, None], (potential_block[:, None, :] - block_cost) / entropy, -jnp.inf)
                partial_value = fold_blocks(scores, row_ids, SB_DEV, 2)
                running = partial_value if running is None else combine(running, partial_value)
            return entropy * log_mass - entropy * (running[0].reshape(-1) + jnp.log(running[1].reshape(-1)))
        return lax.map(per_source, (sources, source_log, pairs, counts))

    def col_update(row_pot):
        def per_source(running, inputs):
            embeddings, potential, slot_lists, live = inputs
            updated = []
            for target in range(N_TGT):
                block_cost, row_ids, col_ids, is_valid, tgt_blocks = block_costs(embeddings, targets[target], slot_lists[target], live[target])
                potential_block = potential.reshape(SB_DEV, BLOCK)[row_ids]
                scores = jnp.where(is_valid[:, None, None], (potential_block[:, :, None] - block_cost) / entropy, -jnp.inf)
                maxima, sumexp = fold_blocks(scores, col_ids, TB_DEV, 1)
                updated.append(combine((running[0][target], running[1][target]), (maxima.reshape(-1), sumexp.reshape(-1))))
            return (jnp.stack([item[0] for item in updated]), jnp.stack([item[1] for item in updated])), None
        initial = (jnp.full((N_TGT, TB_DEV * BLOCK), -jnp.inf, jnp.float32), jnp.zeros((N_TGT, TB_DEV * BLOCK), jnp.float32))
        (maxima, sumexp), unused = lax.scan(per_source, initial, (sources, row_pot, pairs, counts))
        return entropy * target_log - entropy * (maxima + jnp.log(sumexp))

    for iteration in range(ITERS):
        row_pot = row_update(col_pot)
        col_pot = col_update(row_pot)

    def per_map(inputs):
        embeddings, slot_lists, live = inputs
        saved = []
        peak_value = None
        for target in range(N_TGT):
            block_cost, row_ids, col_ids, is_valid, tgt_blocks = block_costs(embeddings, targets[target], slot_lists[target], live[target])
            potential_block = col_pot[target].reshape(TB_DEV, BLOCK)[col_ids]
            scores = jnp.where(is_valid[:, None, None], (potential_block[:, None, :] - block_cost) / entropy, -jnp.inf)
            maxima, onehot = group_max(scores, row_ids, SB_DEV, 2)
            peak_value = maxima if peak_value is None else jnp.maximum(peak_value, maxima)
            saved.append((scores, row_ids, tgt_blocks))
        numerator = jnp.zeros((SB_DEV, BLOCK, emb_width), jnp.float32)
        denominator = jnp.zeros((SB_DEV, BLOCK), jnp.float32)
        for scores, row_ids, tgt_blocks in saved:
            rounded = jnp.exp(scores - peak_value[row_ids][:, :, None]).astype(jnp.bfloat16)
            weights = lax.optimization_barrier(rounded).astype(jnp.float32)
            products = jnp.einsum("bij,bjd->bid", weights, tgt_blocks, precision=lax.Precision.HIGHEST)
            numerator = numerator + jax.ops.segment_sum(products, row_ids, SB_DEV)
            denominator = denominator + jax.ops.segment_sum(jnp.sum(weights, axis=2), row_ids, SB_DEV)
        return (numerator / denominator[:, :, None]).reshape(SB_DEV * BLOCK, emb_width)

    mapped = lax.map(per_map, (sources, pairs, counts)).reshape(N_SRC * SB_DEV * BLOCK, emb_width)
    return row_pot.reshape(-1), col_pot.reshape(-1), mapped
```

```python
import functools

import jax
import jax.numpy as jnp
from jax import lax
from jax.experimental import pallas as pl
from jax.experimental.pallas import tpu as pltpu
from jax.sharding import Mesh
from jax.sharding import PartitionSpec as P

BLOCK = 128
ITERS = 3
SB = 4
TB = 16
MAXB = 32
E = 256
XC = 8
Z = 16
EPS = 0.02
SRC = ("z", "x", "c")


VMEM = pl.BlockSpec(memory_space=pltpu.VMEM)
SMEM = pl.BlockSpec(memory_space=pltpu.SMEM)


def call(kernel, out_shape, scratch, name, flops=1000000, smem=0, vmem=0):
    return pl.pallas_call(
        kernel,
        out_shape=out_shape,
        in_specs=[SMEM] * smem + [VMEM] * vmem,
        out_specs=jax.tree.map(lambda unused: VMEM, out_shape),
        scratch_shapes=scratch,
        compiler_params=pltpu.CompilerParams(vmem_limit_bytes=16 * 1024 * 1024),
        cost_estimate=pl.CostEstimate(flops=flops, bytes_accessed=2000000, transcendentals=500000),
        name=name,
    )


def f32(*shape):
    return jax.ShapeDtypeStruct(shape, jnp.float32)


def entry(pairs, k):
    value = pairs[k]
    return value >> 4, value & 15


def turned(block):
    return jnp.transpose(block, (1, 0))


def log_sum(parts):
    top = jnp.max(parts, axis=0)
    return top + jnp.log(jnp.sum(jnp.exp(parts - top[None]), axis=0))


def row_peaks(peaks):
    for p in range(SB):
        peaks[p] = jnp.broadcast_to(jnp.max(peaks[p], axis=1, keepdims=True), (BLOCK, BLOCK))


def row_partials(peaks, sums):
    found = []
    for p in range(SB):
        total = jnp.sum(turned(sums[p]), axis=0, keepdims=True)
        found.append(turned(peaks[p])[0:1] + jnp.log(total))
    return jnp.concatenate(found, axis=0)


def cost_kernel(pairs, counts, x, y, cost, partial, x_norm, y_norm, peaks, sums):
    live = counts[0]
    for p in range(SB):
        wide = x[pl.ds(p * BLOCK, BLOCK), :].astype(jnp.float32)
        x_norm[p] = jnp.broadcast_to(jnp.sum(wide * wide, axis=1, keepdims=True), (BLOCK, BLOCK))
    ones = jnp.ones((8, E), jnp.bfloat16)
    dims = (((1,), (1,)), ((), ()))

    def norms(q, unused):
        wide = y[pl.ds(pl.multiple_of(q * BLOCK, BLOCK), BLOCK), :].astype(jnp.float32)
        square = wide * wide
        high = square.astype(jnp.bfloat16)
        low = (square - high.astype(jnp.float32)).astype(jnp.bfloat16)
        y_norm[q] = lax.dot_general(
            ones, high, dims, preferred_element_type=jnp.float32
        ) + lax.dot_general(ones, low, dims, preferred_element_type=jnp.float32)
        return unused

    lax.fori_loop(0, TB, norms, 0)
    peaks[...] = jnp.full(peaks.shape, -jnp.inf, jnp.float32)
    sums[...] = jnp.zeros(sums.shape, jnp.float32)

    def first(k, unused):
        p, q = entry(pairs, k)
        xs = x[pl.ds(pl.multiple_of(p * BLOCK, BLOCK), BLOCK), :]
        ys = y[pl.ds(pl.multiple_of(q * BLOCK, BLOCK), BLOCK), :]
        crossed = lax.dot_general(xs, ys, dims, preferred_element_type=jnp.float32)
        block = (x_norm[p] + y_norm[q][0:1] - 2.0 * crossed) * (1.0 / (E * EPS))
        cost[k] = block
        peaks[p] = jnp.maximum(peaks[p], -block)
        return unused

    lax.fori_loop(0, live, first, 0)
    row_peaks(peaks)

    def second(k, unused):
        p, q = entry(pairs, k)
        sums[p] += jnp.exp(-cost[k] - peaks[p])
        return unused

    lax.fori_loop(0, live, second, 0)
    found = row_partials(peaks, sums)
    for d in range(SB):
        partial[d] = found


def col_kernel(pairs, counts, cost, partials, mass, partial, row_pot, spread, peaks, sums):
    live = counts[0]
    potential = jnp.log(mass[...]) - log_sum(partials[...])
    row_pot[...] = EPS * potential
    for p in range(SB):
        spread[p] = turned(jnp.broadcast_to(potential[p : p + 1], (BLOCK, BLOCK)))
    peaks[...] = jnp.full(peaks.shape, -jnp.inf, jnp.float32)
    sums[...] = jnp.zeros(sums.shape, jnp.float32)

    def first(k, unused):
        p, q = entry(pairs, k)
        score = (spread[p] - cost[k]).reshape(BLOCK // 8, 8, BLOCK)
        peaks[q] = jnp.maximum(peaks[q], jnp.max(score, axis=0))
        return unused

    lax.fori_loop(0, live, first, 0)
    peaks[...] = jnp.broadcast_to(jnp.max(peaks[...], axis=1, keepdims=True), peaks.shape)

    def second(k, unused):
        p, q = entry(pairs, k)
        score = (spread[p] - cost[k]).reshape(BLOCK // 8, 8, BLOCK)
        sums[q] += jnp.sum(jnp.exp(score - peaks[q][None]), axis=0)
        return unused

    lax.fori_loop(0, live, second, 0)
    found = peaks[...][:, 0] + jnp.log(jnp.sum(sums[...], axis=1))
    for d in range(XC):
        partial[d] = found


def merge_kernel(partials, merged):
    found = log_sum(partials[...])
    merged[...] = jnp.broadcast_to(found[None], merged.shape)


def spread_col(partials, mass, spread):
    potential = jnp.log(mass[...]) - log_sum(partials[...])
    for q in range(TB):
        spread[q] = jnp.broadcast_to(potential[q : q + 1], (8, BLOCK))
    return potential


def row_scores(cost, spread, k, q):
    score = spread[q][None] - cost[k].reshape(BLOCK // 8, 8, BLOCK)
    return score.reshape(BLOCK, BLOCK)


def row_passes(pairs, live, cost, spread, peaks, sums, also):
    peaks[...] = jnp.full(peaks.shape, -jnp.inf, jnp.float32)
    sums[...] = jnp.zeros(sums.shape, jnp.float32)

    def first(k, unused):
        p, q = entry(pairs, k)
        peaks[p] = jnp.maximum(peaks[p], row_scores(cost, spread, k, q))
        return unused

    lax.fori_loop(0, live, first, 0)
    row_peaks(peaks)

    def second(k, unused):
        p, q = entry(pairs, k)
        weight = jnp.exp(row_scores(cost, spread, k, q) - peaks[p])
        sums[p] += weight
        also(p, q, weight)
        return unused

    lax.fori_loop(0, live, second, 0)


def row_kernel(pairs, counts, cost, partials, mass, partial, spread, peaks, sums):
    spread_col(partials, mass, spread)
    row_passes(pairs, counts[0], cost, spread, peaks, sums, lambda p, q, weight: None)
    found = row_partials(peaks, sums)
    for d in range(SB):
        partial[d] = found


def map_kernel(pairs, counts, cost, partials, mass, y, packet, col_pot, spread, peaks, sums, total):
    potential = spread_col(partials, mass, spread)
    col_pot[...] = EPS * potential
    total[...] = jnp.zeros(total.shape, jnp.float32)

    def also(p, q, weight):
        ys = y[pl.ds(pl.multiple_of(q * BLOCK, BLOCK), BLOCK), :]
        high = weight.astype(jnp.bfloat16)
        low = (weight - high.astype(jnp.float32)).astype(jnp.bfloat16)
        total[p] += jnp.dot(high, ys, preferred_element_type=jnp.float32) + jnp.dot(
            low, ys, preferred_element_type=jnp.float32
        )

    row_passes(pairs, counts[0], cost, spread, peaks, sums, also)
    found = row_partials(peaks, sums)
    for p in range(SB):
        packet[p, pl.ds(0, BLOCK), :] = total[p] / jnp.sum(sums[p], axis=1, keepdims=True)
        packet[p, pl.ds(BLOCK, 8), :] = jnp.concatenate(
            [jnp.broadcast_to(found[p : p + 1], (8, BLOCK))] * 2, axis=1
        )


def mix_kernel(packets, mapped):
    parts = jnp.concatenate([packets[t, pl.ds(BLOCK, 1), pl.ds(0, BLOCK)] for t in range(SB)])
    share = jnp.exp(parts - jnp.max(parts, axis=0, keepdims=True))
    share = share / jnp.sum(share, axis=0, keepdims=True)
    total = jnp.zeros((BLOCK, E), jnp.float32)
    for t in range(SB):
        factor = turned(jnp.broadcast_to(share[t : t + 1], (BLOCK, BLOCK)))
        total = total + jnp.concatenate([factor, factor], axis=1) * packets[t, pl.ds(0, BLOCK), :]
    mapped[...] = jnp.broadcast_to(total[None], mapped.shape)


def shards(source_cells, target_cells, source_mass, target_mass, pairs, counts):
    pairs = pairs.reshape(MAXB)
    counts = counts.reshape(1)
    source_mass = source_mass.reshape(SB, BLOCK)
    target_mass = target_mass.reshape(TB, BLOCK)
    tall = pltpu.VMEM((SB, BLOCK, BLOCK), jnp.float32)
    flat = pltpu.VMEM((TB, 8, BLOCK), jnp.float32)
    cost, row_part = call(
        cost_kernel,
        (f32(MAXB, BLOCK, BLOCK), f32(SB, SB, BLOCK)),
        [tall, flat, tall, tall],
        "cost",
        smem=2,
        vmem=2,
    )(pairs, counts, source_cells, target_cells)
    for iteration in range(ITERS):
        row_parts = lax.all_to_all(row_part, "t", 0, 0)
        col_part, row_pot = call(
            col_kernel,
            (f32(XC, TB, BLOCK), f32(SB, BLOCK)),
            [tall, flat, flat],
            "cols",
            smem=2,
            vmem=3,
        )(pairs, counts, cost, row_parts, source_mass)
        col_parts = lax.all_to_all(col_part, ("x", "c"), 0, 0)
        col_parts = call(merge_kernel, f32(Z, TB, BLOCK), [], "merge", vmem=1)(col_parts)
        col_parts = lax.all_to_all(col_parts, "z", 0, 0)
        if iteration < ITERS - 1:
            row_part = call(
                row_kernel, f32(SB, SB, BLOCK), [flat, tall, tall], "rows", smem=2, vmem=3
            )(pairs, counts, cost, col_parts, target_mass)
    packet, col_pot = call(
        map_kernel,
        (f32(SB, BLOCK + 8, E), f32(TB, BLOCK)),
        [flat, tall, tall, pltpu.VMEM((SB, BLOCK, E), jnp.float32)],
        "mapping",
        smem=2,
        vmem=4,
    )(pairs, counts, cost, col_parts, target_mass, target_cells)
    packets = lax.all_to_all(packet, "t", 0, 0)
    quarters = call(mix_kernel, f32(SB, BLOCK, E), [], "mix", vmem=1)(packets)
    mapped = lax.all_to_all(quarters, "t", 0, 0)
    return row_pot.reshape(-1), col_pot.reshape(-1), mapped.reshape(SB * BLOCK, E)


def solution(mesh):
    fine = Mesh(mesh.devices.reshape(Z, 4, 2, 4), ("z", "x", "c", "t"))
    return jax.shard_map(
        shards,
        mesh=fine,
        in_specs=(P(SRC, None), P("t", None), P(SRC), P("t"), P(SRC, "t", None), P(SRC, "t")),
        out_specs=(P(SRC), P("t"), P(SRC, None)),
        check_vma=False,
    )
```

```python
import jax
import jax.numpy as jnp
from jax import lax
from jax.experimental import pallas as pl
from jax.experimental.pallas import tpu as pltpu
from jax.sharding import Mesh
from jax.sharding import PartitionSpec as P

BLOCK = 128
ITERS = 3
SB = 4
TB = 16
MAXB = 32
E = 256
XC = 8
Z = 16
EPS = 0.02
SRC = ("z", "x", "c")


VMEM = pl.BlockSpec(memory_space=pltpu.VMEM)
ANY = pl.BlockSpec(memory_space=pl.ANY)
OFFSET = 70.0
LEAST = 1e-28
MOST = 1e37
FIRST_LIMIT = 52


def call(kernel, out_shape, scratch, name, specs, out_specs=None):
    return pl.pallas_call(
        kernel,
        out_shape=out_shape,
        in_specs=specs,
        out_specs=out_specs or jax.tree.map(lambda unused: VMEM, out_shape),
        scratch_shapes=scratch,
        compiler_params=pltpu.CompilerParams(vmem_limit_bytes=16 * 1024 * 1024),
        cost_estimate=pl.CostEstimate(flops=1000000, bytes_accessed=2000000, transcendentals=500000),
        name=name,
    )


def f32(*shape):
    return jax.ShapeDtypeStruct(shape, jnp.float32)


def fetch(pairs_hbm, counts_hbm, pairs, counts, done):
    copies = [
        pltpu.make_async_copy(pairs_hbm, pairs, done.at[0]),
        pltpu.make_async_copy(counts_hbm, counts, done.at[1]),
    ]
    for copy in copies:
        copy.start()
    return copies


def fetched(copies, counts):
    for copy in copies:
        copy.wait()
    return counts[0]


def entry(pairs, k):
    value = pairs[k]
    return value >> 4, value & 15


def turned(block):
    return jnp.transpose(block, (1, 0))


def log_sum(parts):
    top = jnp.max(parts, axis=0)
    return top + jnp.log(jnp.sum(jnp.exp(parts - top[None]), axis=0))


def in_range(totals):
    return jnp.logical_and(jnp.min(totals) >= LEAST, jnp.max(totals) <= MOST)


def spread_rows(potential, spread):
    for p in range(SB):
        spread[p] = turned(jnp.broadcast_to(potential[p : p + 1], (BLOCK, BLOCK)))


def spread_cols(potential, spread):
    for q in range(TB):
        spread[q] = jnp.broadcast_to(potential[q : q + 1], (8, BLOCK))


def row_scores(gram, spread, p, q):
    score = spread[q][None] + gram[p, q].reshape(BLOCK // 8, 8, BLOCK)
    return score.reshape(BLOCK, BLOCK)


def row_totals(sums):
    return jnp.concatenate(
        [jnp.sum(turned(sums[p]), axis=0, keepdims=True) for p in range(SB)], axis=0
    )


def row_passes(pairs, live, gram, spread, peaks, sums, found, also):
    peaks[...] = jnp.full(peaks.shape, -jnp.inf, jnp.float32)
    sums[...] = jnp.zeros(sums.shape, jnp.float32)

    def first(k, unused):
        p, q = entry(pairs, k)
        peaks[p] = jnp.maximum(peaks[p], row_scores(gram, spread, p, q))
        return unused

    lax.fori_loop(0, live, first, 0)
    for p in range(SB):
        peaks[p] = jnp.broadcast_to(jnp.max(peaks[p], axis=1, keepdims=True), (BLOCK, BLOCK))

    def second(k, unused):
        p, q = entry(pairs, k)
        weight = jnp.exp(row_scores(gram, spread, p, q) - peaks[p])
        sums[p] += weight
        also(p, q, weight)
        return unused

    lax.fori_loop(0, live, second, 0)
    tops = jnp.concatenate([turned(peaks[p])[0:1] for p in range(SB)], axis=0)
    found[...] = tops + jnp.log(row_totals(sums))


def row_pass(pairs, live, gram, spread, before, row_spread, sums, found, peaks, also):
    sums[...] = jnp.zeros(sums.shape, jnp.float32)

    def only(k, unused):
        p, q = entry(pairs, k)
        weight = jnp.exp(row_scores(gram, spread, p, q) + row_spread[p])
        sums[p] += weight
        also(p, q, weight)
        return unused

    lax.fori_loop(0, live, only, 0)
    totals = row_totals(sums)
    found[...] = jnp.log(totals) - (before + OFFSET)

    @pl.when(jnp.logical_not(in_range(totals)))
    def again():
        row_passes(pairs, live, gram, spread, peaks, sums, found, also)


def folded(cells):
    wide = cells.astype(jnp.float32)
    square = wide * wide
    square = turned(square[:, :BLOCK] + square[:, BLOCK:])
    return jnp.sum(square, axis=0, keepdims=True) * (1.0 / (E * EPS))


def nothing(p, q, weight):
    return None


def gram_kernel(
    pairs_hbm,
    counts_hbm,
    x,
    y,
    gram,
    partial,
    x_norm,
    y_norm,
    pairs,
    counts,
    done,
    spread,
    row_spread,
    peaks,
    sums,
    found,
):
    lists = fetch(pairs_hbm, counts_hbm, pairs, counts, done)
    for p in range(SB):
        x_norm[pl.ds(p, 1)] = folded(x[pl.ds(p * BLOCK, BLOCK), :])

    def chunk(c, unused):
        cells = y[pl.ds(pl.multiple_of(c * 2 * BLOCK, 2 * BLOCK), 2 * BLOCK), :]
        dims = (((1,), (1,)), ((), ()))
        crossed = lax.dot_general(x[...], cells, dims, preferred_element_type=jnp.float32)
        crossed = crossed * (2.0 / (E * EPS))
        for half in range(2):
            norm = folded(cells[half * BLOCK : (half + 1) * BLOCK])
            spread[2 * c + half] = jnp.broadcast_to(-norm, (8, BLOCK))
            for p in range(SB):
                gram[p, 2 * c + half] = crossed[
                    p * BLOCK : (p + 1) * BLOCK, half * BLOCK : (half + 1) * BLOCK
                ]
        return unused

    lax.fori_loop(0, TB // 2, chunk, 0)
    y_norm[...] = -spread[...][:, 0]
    before = -x_norm[...]
    spread_rows(before + OFFSET, row_spread)
    live = fetched(lists, counts)
    row_pass(pairs, live, gram, spread, before, row_spread, sums, found, peaks, nothing)
    for d in range(SB):
        partial[d] = found[...]


def col_kernel(
    pairs_hbm,
    counts_hbm,
    gram,
    partials,
    mass,
    before,
    partial,
    potential,
    pairs,
    counts,
    done,
    spread,
    col_spread,
    peaks,
    sums,
    found,
):
    lists = fetch(pairs_hbm, counts_hbm, pairs, counts, done)
    potential[...] = jnp.log(mass[...]) - log_sum(partials[...])
    spread_rows(potential[...], spread)
    spread_cols(before[...] + OFFSET, col_spread)
    sums[...] = jnp.zeros(sums.shape, jnp.float32)
    live = fetched(lists, counts)

    def scores(p, q):
        return (spread[p] + gram[p, q]).reshape(BLOCK // 8, 8, BLOCK)

    def only(k, unused):
        p, q = entry(pairs, k)
        sums[q] += jnp.sum(jnp.exp(scores(p, q) + col_spread[q][None]), axis=0)
        return unused

    lax.fori_loop(0, live, only, 0)
    totals = jnp.sum(sums[...], axis=1)
    found[...] = jnp.log(totals) - (before[...] + OFFSET)

    @pl.when(jnp.logical_not(in_range(totals)))
    def again():
        peaks[...] = jnp.full(peaks.shape, -jnp.inf, jnp.float32)
        sums[...] = jnp.zeros(sums.shape, jnp.float32)

        def first(k, unused):
            p, q = entry(pairs, k)
            peaks[q] = jnp.maximum(peaks[q], jnp.max(scores(p, q), axis=0))
            return unused

        lax.fori_loop(0, live, first, 0)
        peaks[...] = jnp.broadcast_to(jnp.max(peaks[...], axis=1, keepdims=True), peaks.shape)

        def second(k, unused):
            p, q = entry(pairs, k)
            sums[q] += jnp.sum(jnp.exp(scores(p, q) - peaks[q][None]), axis=0)
            return unused

        lax.fori_loop(0, live, second, 0)
        found[...] = peaks[...][:, 0] + jnp.log(jnp.sum(sums[...], axis=1))

    for d in range(XC):
        partial[d] = found[...]


def merge_kernel(partials, merged):
    found = log_sum(partials[...])
    merged[...] = jnp.broadcast_to(found[None], merged.shape)


def row_kernel(
    pairs_hbm,
    counts_hbm,
    gram,
    partials,
    mass,
    before,
    partial,
    potential,
    pairs,
    counts,
    done,
    spread,
    row_spread,
    peaks,
    sums,
    found,
):
    lists = fetch(pairs_hbm, counts_hbm, pairs, counts, done)
    potential[...] = jnp.log(mass[...]) - log_sum(partials[...])
    spread_cols(potential[...], spread)
    spread_rows(before[...] + OFFSET, row_spread)
    live = fetched(lists, counts)
    row_pass(
        pairs, live, gram, spread, before[...], row_spread, sums, found, peaks, nothing
    )
    for d in range(SB):
        partial[d] = found[...]


def map_kernel(
    pairs_hbm,
    counts_hbm,
    gram,
    partials,
    mass,
    before,
    x_norm,
    y_norm,
    y,
    packet,
    row_pot,
    col_pot,
    pairs,
    counts,
    done,
    spread,
    row_spread,
    peaks,
    sums,
    found,
    high,
    low,
    rows_out,
    cols_out,
):
    lists = fetch(pairs_hbm, counts_hbm, pairs, counts, done)
    potential = jnp.log(mass[...]) - log_sum(partials[...])
    rows_out[...] = EPS * (before[...] + x_norm[...])
    cols_out[...] = EPS * (potential + y_norm[...])
    copies = [
        pltpu.make_async_copy(rows_out, row_pot, done.at[2]),
        pltpu.make_async_copy(cols_out, col_pot, done.at[3]),
    ]
    for copy in copies:
        copy.start()
    spread_cols(potential, spread)
    spread_rows(before[...] + OFFSET, row_spread)
    high[...] = jnp.zeros(high.shape, jnp.bfloat16)
    low[...] = jnp.zeros(low.shape, jnp.bfloat16)

    def also(p, q, weight):
        rows = pl.ds(pl.multiple_of(p * BLOCK, BLOCK), BLOCK)
        cols = pl.ds(pl.multiple_of(q * BLOCK, BLOCK), BLOCK)
        leading = weight.astype(jnp.bfloat16)
        high[rows, cols] = leading
        low[rows, cols] = (weight - leading.astype(jnp.float32)).astype(jnp.bfloat16)

    live = fetched(lists, counts)
    row_pass(pairs, live, gram, spread, before[...], row_spread, sums, found, peaks, also)
    total = jnp.dot(high[...], y[...], preferred_element_type=jnp.float32) + jnp.dot(
        low[...], y[...], preferred_element_type=jnp.float32
    )
    for p in range(SB):
        packet[p, pl.ds(0, BLOCK), :] = total[p * BLOCK : (p + 1) * BLOCK] / jnp.sum(
            sums[p], axis=1, keepdims=True
        )
        packet[p, pl.ds(BLOCK, 8), :] = jnp.concatenate(
            [jnp.broadcast_to(found[pl.ds(p, 1)], (8, BLOCK))] * 2, axis=1
        )
    for copy in copies:
        copy.wait()


def mix_kernel(packets, mapped):
    parts = jnp.concatenate([packets[t, pl.ds(BLOCK, 1), pl.ds(0, BLOCK)] for t in range(SB)])
    share = jnp.exp(parts - jnp.max(parts, axis=0, keepdims=True))
    share = share / jnp.sum(share, axis=0, keepdims=True)
    total = jnp.zeros((BLOCK, E), jnp.float32)
    for t in range(SB):
        factor = turned(jnp.broadcast_to(share[t : t + 1], (BLOCK, BLOCK)))
        total = total + jnp.concatenate([factor, factor], axis=1) * packets[t, pl.ds(0, BLOCK), :]
    mapped[...] = jnp.broadcast_to(total[None], mapped.shape)


def shards(source_cells, target_cells, source_mass, target_mass, pairs, counts):
    pairs = pairs.reshape(MAXB)
    counts = counts.reshape(1)
    source_mass = source_mass.reshape(SB, BLOCK)
    target_mass = target_mass.reshape(TB, BLOCK)
    tall = pltpu.VMEM((SB, BLOCK, BLOCK), jnp.float32)
    flat = pltpu.VMEM((TB, 8, BLOCK), jnp.float32)
    rows = pltpu.VMEM((SB, BLOCK), jnp.float32)
    cols = pltpu.VMEM((TB, BLOCK), jnp.float32)
    dense = pltpu.VMEM((SB * BLOCK, TB * BLOCK), jnp.bfloat16)
    lists = [pltpu.SMEM((MAXB,), jnp.int32), pltpu.SMEM((1,), jnp.int32)]

    def sems(count):
        return pltpu.SemaphoreType.DMA((count,))

    gram, row_part, x_norm, y_norm = call(
        gram_kernel,
        (f32(SB, TB, BLOCK, BLOCK), f32(SB, SB, BLOCK), f32(SB, BLOCK), f32(TB, BLOCK)),
        lists + [sems(2), flat, tall, tall, tall, rows],
        "gram",
        [ANY] * 2 + [VMEM] * 2,
    )(pairs, counts, source_cells, target_cells)
    col_pot = -y_norm
    for iteration in range(ITERS):
        row_parts = lax.all_to_all(row_part, "t", 0, 0)
        col_part, row_pot = call(
            col_kernel,
            (f32(XC, TB, BLOCK), f32(SB, BLOCK)),
            lists + [sems(2), tall, flat, flat, flat, cols],
            "cols",
            [ANY] * 2 + [VMEM] * 4,
        )(pairs, counts, gram, row_parts, source_mass, col_pot)
        col_parts = lax.all_to_all(col_part, ("x", "c"), 0, 0)
        col_parts = call(merge_kernel, f32(Z, TB, BLOCK), [], "merge", [VMEM])(col_parts)
        col_parts = lax.all_to_all(col_parts, "z", 0, 0)
        if iteration < ITERS - 1:
            row_part, col_pot = call(
                row_kernel,
                (f32(SB, SB, BLOCK), f32(TB, BLOCK)),
                lists + [sems(2), flat, tall, tall, tall, rows],
                "rows",
                [ANY] * 2 + [VMEM] * 4,
            )(pairs, counts, gram, col_parts, target_mass, row_pot)
    packet, row_pot, col_pot = call(
        map_kernel,
        (f32(SB, BLOCK + 8, E), f32(SB, BLOCK), f32(TB, BLOCK)),
        lists + [sems(4), flat, tall, tall, tall, rows, dense, dense, rows, cols],
        "mapping",
        [ANY] * 2 + [VMEM] * 7,
        out_specs=(VMEM, ANY, ANY),
    )(pairs, counts, gram, col_parts, target_mass, row_pot, x_norm, y_norm, target_cells)
    packets = lax.all_to_all(packet, "t", 0, 0)
    quarters = call(mix_kernel, f32(SB, BLOCK, E), [], "mix", [VMEM])(packets)
    mapped = lax.all_to_all(quarters, "t", 0, 0)
    return row_pot.reshape(-1), col_pot.reshape(-1), mapped.reshape(SB * BLOCK, E)


def solution(mesh):
    fine = Mesh(mesh.devices.reshape(Z, 4, 2, 4), ("z", "x", "c", "t"))
    return jax.shard_map(
        shards,
        mesh=fine,
        in_specs=(P(SRC, None), P("t", None), P(SRC), P("t"), P(SRC, "t", None), P(SRC, "t")),
        out_specs=(P(SRC), P("t"), P(SRC, None)),
        check_vma=False,
    )
```

```python
import jax
import jax.numpy as jnp
from jax import lax
from jax.experimental import pallas as pl
from jax.experimental.pallas import tpu as pltpu
from jax.sharding import Mesh
from jax.sharding import PartitionSpec as P

BLOCK = 128
ITERS = 3
SB = 4
TB = 16
MAXB = 32
E = 256
XC = 8
Z = 16
EPS = 0.02
SRC = ("z", "x", "c")


VMEM = pl.BlockSpec(memory_space=pltpu.VMEM)
ANY = pl.BlockSpec(memory_space=pl.ANY)
OFFSET = 70.0
ROW_STEP = 4
COL_STEP = 4
LEAST = 1e-28
MOST = 1e37
FIRST_LIMIT = 52


def call(kernel, out_shape, scratch, name, specs, out_specs=None):
    return pl.pallas_call(
        kernel,
        out_shape=out_shape,
        in_specs=specs,
        out_specs=out_specs or jax.tree.map(lambda unused: VMEM, out_shape),
        scratch_shapes=scratch,
        compiler_params=pltpu.CompilerParams(vmem_limit_bytes=16 * 1024 * 1024),
        cost_estimate=pl.CostEstimate(flops=1000000, bytes_accessed=2000000, transcendentals=500000),
        name=name,
    )


def f32(*shape):
    return jax.ShapeDtypeStruct(shape, jnp.float32)


def fetch(pairs_hbm, counts_hbm, pairs, counts, done):
    copies = [
        pltpu.make_async_copy(pairs_hbm, pairs, done.at[0]),
        pltpu.make_async_copy(counts_hbm, counts, done.at[1]),
    ]
    for copy in copies:
        copy.start()
    return copies


def fetched(copies, counts):
    for copy in copies:
        copy.wait()
    return counts[0]


def each(live, step, body):
    whole = live >> (step.bit_length() - 1)

    def several(i, unused):
        body([i * step + j for j in range(step)])
        return unused

    def single(k, unused):
        body([k])
        return unused

    lax.fori_loop(0, whole, several, 0)
    lax.fori_loop(whole * step, live, single, 0)


def entry(pairs, k):
    value = pairs[k]
    return value >> 4, value & 15


def turned(block):
    return jnp.transpose(block, (1, 0))


def log_sum(parts):
    top = jnp.max(parts, axis=0)
    return top + jnp.log(jnp.sum(jnp.exp(parts - top[None]), axis=0))


def in_range(totals):
    return jnp.logical_and(jnp.min(totals) >= LEAST, jnp.max(totals) <= MOST)


def spread_rows(potential, spread):
    for p in range(SB):
        spread[p] = turned(jnp.broadcast_to(potential[p : p + 1], (BLOCK, BLOCK)))


def spread_cols(potential, spread):
    for q in range(TB):
        spread[q] = jnp.broadcast_to(potential[q : q + 1], (8, BLOCK))


def row_scores(gram, spread, p, q):
    score = spread[q][None] + gram[p, q].reshape(BLOCK // 8, 8, BLOCK)
    return score.reshape(BLOCK, BLOCK)


def row_totals(sums):
    return jnp.concatenate(
        [jnp.sum(turned(sums[p]), axis=0, keepdims=True) for p in range(SB)], axis=0
    )


def row_passes(pairs, live, gram, spread, peaks, sums, found, also):
    peaks[...] = jnp.full(peaks.shape, -jnp.inf, jnp.float32)
    sums[...] = jnp.zeros(sums.shape, jnp.float32)

    def first(k, unused):
        p, q = entry(pairs, k)
        peaks[p] = jnp.maximum(peaks[p], row_scores(gram, spread, p, q))
        return unused

    lax.fori_loop(0, live, first, 0)
    for p in range(SB):
        peaks[p] = jnp.broadcast_to(jnp.max(peaks[p], axis=1, keepdims=True), (BLOCK, BLOCK))

    def second(k, unused):
        p, q = entry(pairs, k)
        weight = jnp.exp(row_scores(gram, spread, p, q) - peaks[p])
        sums[p] += weight
        also(p, q, weight)
        return unused

    lax.fori_loop(0, live, second, 0)
    tops = jnp.concatenate([turned(peaks[p])[0:1] for p in range(SB)], axis=0)
    found[...] = tops + jnp.log(row_totals(sums))


def row_pass(pairs, live, gram, spread, before, row_spread, sums, found, peaks, also):
    sums[...] = jnp.zeros(sums.shape, jnp.float32)

    def only(slots):
        places = [entry(pairs, k) for k in slots]
        weights = [jnp.exp(row_scores(gram, spread, p, q) + row_spread[p]) for p, q in places]
        for (p, q), weight in zip(places, weights):
            sums[p] += weight
            also(p, q, weight)

    each(live, ROW_STEP, only)
    totals = row_totals(sums)
    found[...] = jnp.log(totals) - (before + OFFSET)

    @pl.when(jnp.logical_not(in_range(totals)))
    def again():
        row_passes(pairs, live, gram, spread, peaks, sums, found, also)


def folded(cells):
    wide = cells.astype(jnp.float32)
    square = wide * wide
    square = turned(square[:, :BLOCK] + square[:, BLOCK:])
    return jnp.sum(square, axis=0, keepdims=True) * (1.0 / (E * EPS))


def nothing(p, q, weight):
    return None


def gram_kernel(
    pairs_hbm,
    counts_hbm,
    x,
    y,
    gram,
    partial,
    x_norm,
    y_start,
    pairs,
    counts,
    done,
    spread,
    row_spread,
    peaks,
    sums,
    found,
):
    lists = fetch(pairs_hbm, counts_hbm, pairs, counts, done)
    for p in range(SB):
        x_norm[pl.ds(p, 1)] = folded(x[pl.ds(p * BLOCK, BLOCK), :])

    def chunk(c):
        cells = y[pl.ds(c * 2 * BLOCK, 2 * BLOCK), :]
        dims = (((1,), (1,)), ((), ()))
        crossed = lax.dot_general(x[...], cells, dims, preferred_element_type=jnp.float32)
        crossed = crossed * (2.0 / (E * EPS))
        for half in range(2):
            norm = folded(cells[half * BLOCK : (half + 1) * BLOCK])
            spread[2 * c + half] = jnp.broadcast_to(-norm, (8, BLOCK))
            for p in range(SB):
                gram[p, 2 * c + half] = crossed[
                    p * BLOCK : (p + 1) * BLOCK, half * BLOCK : (half + 1) * BLOCK
                ]

    for c in range(TB // 2):
        chunk(c)
    y_start[...] = spread[...][:, 0]
    before = -x_norm[...]
    spread_rows(before + OFFSET, row_spread)
    live = fetched(lists, counts)
    row_pass(pairs, live, gram, spread, before, row_spread, sums, found, peaks, nothing)
    for d in range(SB):
        partial[d] = found[...]


def col_kernel(
    pairs_hbm,
    counts_hbm,
    gram,
    partials,
    mass,
    before,
    partial,
    potential,
    pairs,
    counts,
    done,
    spread,
    col_spread,
    peaks,
    sums,
    found,
):
    lists = fetch(pairs_hbm, counts_hbm, pairs, counts, done)
    potential[...] = jnp.log(mass[...]) - log_sum(partials[...])
    spread_rows(potential[...], spread)
    spread_cols(before[...] + OFFSET, col_spread)
    sums[...] = jnp.zeros(sums.shape, jnp.float32)
    live = fetched(lists, counts)

    def scores(p, q):
        return (spread[p] + gram[p, q]).reshape(BLOCK // 8, 8, BLOCK)

    def only(slots):
        places = [entry(pairs, k) for k in slots]
        parts = [jnp.sum(jnp.exp(scores(p, q) + col_spread[q][None]), axis=0) for p, q in places]
        for (p, q), part in zip(places, parts):
            sums[q] += part

    each(live, COL_STEP, only)
    totals = jnp.sum(sums[...], axis=1)
    found[...] = jnp.log(totals) - (before[...] + OFFSET)

    @pl.when(jnp.logical_not(in_range(totals)))
    def again():
        peaks[...] = jnp.full(peaks.shape, -jnp.inf, jnp.float32)
        sums[...] = jnp.zeros(sums.shape, jnp.float32)

        def first(k, unused):
            p, q = entry(pairs, k)
            peaks[q] = jnp.maximum(peaks[q], jnp.max(scores(p, q), axis=0))
            return unused

        lax.fori_loop(0, live, first, 0)
        peaks[...] = jnp.broadcast_to(jnp.max(peaks[...], axis=1, keepdims=True), peaks.shape)

        def second(k, unused):
            p, q = entry(pairs, k)
            sums[q] += jnp.sum(jnp.exp(scores(p, q) - peaks[q][None]), axis=0)
            return unused

        lax.fori_loop(0, live, second, 0)
        found[...] = peaks[...][:, 0] + jnp.log(jnp.sum(sums[...], axis=1))

    for d in range(XC):
        partial[d] = found[...]


def merge_kernel(partials, merged):
    found = log_sum(partials[...])
    merged[...] = jnp.broadcast_to(found[None], merged.shape)


def row_kernel(
    pairs_hbm,
    counts_hbm,
    gram,
    partials,
    mass,
    before,
    partial,
    potential,
    pairs,
    counts,
    done,
    spread,
    row_spread,
    peaks,
    sums,
    found,
):
    lists = fetch(pairs_hbm, counts_hbm, pairs, counts, done)
    potential[...] = jnp.log(mass[...]) - log_sum(partials[...])
    spread_cols(potential[...], spread)
    spread_rows(before[...] + OFFSET, row_spread)
    live = fetched(lists, counts)
    row_pass(
        pairs, live, gram, spread, before[...], row_spread, sums, found, peaks, nothing
    )
    for d in range(SB):
        partial[d] = found[...]


def map_kernel(
    pairs_hbm,
    counts_hbm,
    gram,
    partials,
    mass,
    before,
    x_norm,
    y_start,
    y,
    packet,
    row_pot,
    col_pot,
    pairs,
    counts,
    done,
    spread,
    row_spread,
    peaks,
    sums,
    found,
    high,
    low,
    rows_out,
    cols_out,
):
    lists = fetch(pairs_hbm, counts_hbm, pairs, counts, done)
    potential = jnp.log(mass[...]) - log_sum(partials[...])
    rows_out[...] = EPS * (before[...] + x_norm[...])
    cols_out[...] = EPS * (potential - y_start[...])
    copies = [
        pltpu.make_async_copy(rows_out, row_pot, done.at[2]),
        pltpu.make_async_copy(cols_out, col_pot, done.at[3]),
    ]
    for copy in copies:
        copy.start()
    spread_cols(potential, spread)
    spread_rows(before[...] + OFFSET, row_spread)
    high[...] = jnp.zeros(high.shape, jnp.bfloat16)
    low[...] = jnp.zeros(low.shape, jnp.bfloat16)

    def also(p, q, weight):
        rows = pl.ds(pl.multiple_of(p * BLOCK, BLOCK), BLOCK)
        cols = pl.ds(pl.multiple_of(q * BLOCK, BLOCK), BLOCK)
        leading = weight.astype(jnp.bfloat16)
        high[rows, cols] = leading
        low[rows, cols] = (weight - leading.astype(jnp.float32)).astype(jnp.bfloat16)

    live = fetched(lists, counts)
    row_pass(pairs, live, gram, spread, before[...], row_spread, sums, found, peaks, also)
    total = jnp.dot(high[...], y[...], preferred_element_type=jnp.float32) + jnp.dot(
        low[...], y[...], preferred_element_type=jnp.float32
    )
    for p in range(SB):
        packet[p, pl.ds(0, BLOCK), :] = total[p * BLOCK : (p + 1) * BLOCK] / jnp.sum(
            sums[p], axis=1, keepdims=True
        )
        packet[p, pl.ds(BLOCK, 8), :] = jnp.concatenate(
            [jnp.broadcast_to(found[pl.ds(p, 1)], (8, BLOCK))] * 2, axis=1
        )
    for copy in copies:
        copy.wait()


def mix_kernel(packets, mapped):
    parts = jnp.concatenate([packets[t, pl.ds(BLOCK, 1), pl.ds(0, BLOCK)] for t in range(SB)])
    share = jnp.exp(parts - jnp.max(parts, axis=0, keepdims=True))
    share = share / jnp.sum(share, axis=0, keepdims=True)
    total = jnp.zeros((BLOCK, E), jnp.float32)
    for t in range(SB):
        factor = turned(jnp.broadcast_to(share[t : t + 1], (BLOCK, BLOCK)))
        total = total + jnp.concatenate([factor, factor], axis=1) * packets[t, pl.ds(0, BLOCK), :]
    mapped[...] = jnp.broadcast_to(total[None], mapped.shape)


def shards(source_cells, target_cells, source_mass, target_mass, pairs, counts):
    pairs = pairs.reshape(MAXB)
    counts = counts.reshape(1)
    source_mass = source_mass.reshape(SB, BLOCK)
    target_mass = target_mass.reshape(TB, BLOCK)
    tall = pltpu.VMEM((SB, BLOCK, BLOCK), jnp.float32)
    flat = pltpu.VMEM((TB, 8, BLOCK), jnp.float32)
    rows = pltpu.VMEM((SB, BLOCK), jnp.float32)
    cols = pltpu.VMEM((TB, BLOCK), jnp.float32)
    dense = pltpu.VMEM((SB * BLOCK, TB * BLOCK), jnp.bfloat16)
    lists = [pltpu.SMEM((MAXB,), jnp.int32), pltpu.SMEM((1,), jnp.int32)]

    def sems(count):
        return pltpu.SemaphoreType.DMA((count,))

    gram, row_part, x_norm, y_start = call(
        gram_kernel,
        (f32(SB, TB, BLOCK, BLOCK), f32(SB, SB, BLOCK), f32(SB, BLOCK), f32(TB, BLOCK)),
        lists + [sems(2), flat, tall, tall, tall, rows],
        "gram",
        [ANY] * 2 + [VMEM] * 2,
    )(pairs, counts, source_cells, target_cells)
    col_pot = y_start
    for iteration in range(ITERS):
        row_parts = lax.all_to_all(row_part, "t", 0, 0)
        col_part, row_pot = call(
            col_kernel,
            (f32(XC, TB, BLOCK), f32(SB, BLOCK)),
            lists + [sems(2), tall, flat, flat, flat, cols],
            "cols",
            [ANY] * 2 + [VMEM] * 4,
        )(pairs, counts, gram, row_parts, source_mass, col_pot)
        col_parts = lax.all_to_all(col_part, ("x", "c"), 0, 0)
        col_parts = call(merge_kernel, f32(Z, TB, BLOCK), [], "merge", [VMEM])(col_parts)
        col_parts = lax.all_to_all(col_parts, "z", 0, 0)
        if iteration < ITERS - 1:
            row_part, col_pot = call(
                row_kernel,
                (f32(SB, SB, BLOCK), f32(TB, BLOCK)),
                lists + [sems(2), flat, tall, tall, tall, rows],
                "rows",
                [ANY] * 2 + [VMEM] * 4,
            )(pairs, counts, gram, col_parts, target_mass, row_pot)
    packet, row_pot, col_pot = call(
        map_kernel,
        (f32(SB, BLOCK + 8, E), f32(SB, BLOCK), f32(TB, BLOCK)),
        lists + [sems(4), flat, tall, tall, tall, rows, dense, dense, rows, cols],
        "mapping",
        [ANY] * 2 + [VMEM] * 7,
        out_specs=(VMEM, ANY, ANY),
    )(pairs, counts, gram, col_parts, target_mass, row_pot, x_norm, y_start, target_cells)
    packets = lax.all_to_all(packet, "t", 0, 0)
    quarters = call(mix_kernel, f32(SB, BLOCK, E), [], "mix", [VMEM])(packets)
    mapped = lax.all_to_all(quarters, "t", 0, 0)
    return row_pot.reshape(-1), col_pot.reshape(-1), mapped.reshape(SB * BLOCK, E)


def solution(mesh):
    fine = Mesh(mesh.devices.reshape(Z, 4, 2, 4), ("z", "x", "c", "t"))
    return jax.shard_map(
        shards,
        mesh=fine,
        in_specs=(P(SRC, None), P("t", None), P(SRC), P("t"), P(SRC, "t", None), P(SRC, "t")),
        out_specs=(P(SRC), P("t"), P(SRC, None)),
        check_vma=False,
    )
```

```python
import jax
import jax.numpy as jnp
from jax import lax
from jax.experimental import pallas as pl
from jax.experimental.pallas import tpu as pltpu
from jax.sharding import Mesh
from jax.sharding import PartitionSpec as P

BLOCK = 128
ITERS = 3
SB = 4
TB = 16
MAXB = 32
E = 256
XC = 8
Z = 16
EPS = 0.02
SRC = ("z", "x", "c")


VMEM = pl.BlockSpec(memory_space=pltpu.VMEM)
ANY = pl.BlockSpec(memory_space=pl.ANY)
OFFSET = 70.0
FIRST = 5000000000
ROW_STEP = 4
COL_STEP = 4
LEAST = 1e-28
MOST = 1e37
FIRST_LIMIT = 52


def call(kernel, out_shape, scratch, name, specs, out_specs=None, flops=1000000):
    return pl.pallas_call(
        kernel,
        out_shape=out_shape,
        in_specs=specs,
        out_specs=out_specs or jax.tree.map(lambda unused: VMEM, out_shape),
        scratch_shapes=scratch,
        compiler_params=pltpu.CompilerParams(vmem_limit_bytes=16 * 1024 * 1024),
        cost_estimate=pl.CostEstimate(flops=flops, bytes_accessed=2000000, transcendentals=500000),
        name=name,
    )


def f32(*shape):
    return jax.ShapeDtypeStruct(shape, jnp.float32)


def fetch(pairs_hbm, counts_hbm, pairs, counts, done):
    copies = [
        pltpu.make_async_copy(pairs_hbm, pairs, done.at[0]),
        pltpu.make_async_copy(counts_hbm, counts, done.at[1]),
    ]
    for copy in copies:
        copy.start()
    return copies


def fetched(copies, counts):
    for copy in copies:
        copy.wait()
    return counts[0]


def each(live, step, body):
    whole = live >> (step.bit_length() - 1)

    def several(i, unused):
        body([i * step + j for j in range(step)])
        return unused

    def single(k, unused):
        body([k])
        return unused

    lax.fori_loop(0, whole, several, 0)
    lax.fori_loop(whole * step, live, single, 0)


def entry(pairs, k):
    value = pairs[k]
    return value >> 4, value & 15


def turned(block):
    return jnp.transpose(block, (1, 0))


def log_sum(parts):
    top = jnp.max(parts, axis=0)
    return top + jnp.log(jnp.sum(jnp.exp(parts - top[None]), axis=0))


def in_range(totals):
    return jnp.logical_and(jnp.min(totals) >= LEAST, jnp.max(totals) <= MOST)


def spread_rows(potential, spread):
    for p in range(SB):
        spread[p] = turned(jnp.broadcast_to(potential[p : p + 1], (BLOCK, BLOCK)))


def spread_cols(potential, spread):
    for q in range(TB):
        spread[q] = jnp.broadcast_to(potential[q : q + 1], (8, BLOCK))


def row_scores(gram, spread, p, q):
    score = spread[q][None] + gram[p, q].reshape(BLOCK // 8, 8, BLOCK)
    return score.reshape(BLOCK, BLOCK)


def row_totals(sums):
    return jnp.concatenate(
        [jnp.sum(turned(sums[p]), axis=0, keepdims=True) for p in range(SB)], axis=0
    )


def row_passes(pairs, live, gram, spread, peaks, sums, found, also):
    peaks[...] = jnp.full(peaks.shape, -jnp.inf, jnp.float32)
    sums[...] = jnp.zeros(sums.shape, jnp.float32)

    def first(k, unused):
        p, q = entry(pairs, k)
        peaks[p] = jnp.maximum(peaks[p], row_scores(gram, spread, p, q))
        return unused

    lax.fori_loop(0, live, first, 0)
    for p in range(SB):
        peaks[p] = jnp.broadcast_to(jnp.max(peaks[p], axis=1, keepdims=True), (BLOCK, BLOCK))

    def second(k, unused):
        p, q = entry(pairs, k)
        weight = jnp.exp(row_scores(gram, spread, p, q) - peaks[p])
        sums[p] += weight
        also(p, q, weight)
        return unused

    lax.fori_loop(0, live, second, 0)
    tops = jnp.concatenate([turned(peaks[p])[0:1] for p in range(SB)], axis=0)
    found[...] = tops + jnp.log(row_totals(sums))


def row_pass(pairs, live, gram, spread, before, row_spread, sums, found, peaks, also):
    sums[...] = jnp.zeros(sums.shape, jnp.float32)

    def only(slots):
        places = [entry(pairs, k) for k in slots]
        weights = [jnp.exp(row_scores(gram, spread, p, q) + row_spread[p]) for p, q in places]
        for (p, q), weight in zip(places, weights):
            sums[p] += weight
            also(p, q, weight)

    each(live, ROW_STEP, only)
    totals = row_totals(sums)
    found[...] = jnp.log(totals) - (before + OFFSET)

    @pl.when(jnp.logical_not(in_range(totals)))
    def again():
        row_passes(pairs, live, gram, spread, peaks, sums, found, also)


def folded(cells):
    wide = cells.astype(jnp.float32)
    square = wide * wide
    square = turned(square[:, :BLOCK] + square[:, BLOCK:])
    return jnp.sum(square, axis=0, keepdims=True) * (1.0 / (E * EPS))


def nothing(p, q, weight):
    return None


def zero_kernel(zeros):
    zeros[...] = jnp.zeros(zeros.shape, jnp.float32)


def gram_kernel(
    pairs_hbm,
    counts_hbm,
    x,
    y,
    mass,
    zeros,
    gram,
    partial,
    x_norm,
    y_start,
    log_mass,
    pairs,
    counts,
    done,
    spread,
    row_spread,
    peaks,
    sums,
    found,
):
    log_mass[...] = jnp.log(mass[...])
    lists = fetch(pairs_hbm, counts_hbm, pairs, counts, done)
    for p in range(SB):
        x_norm[pl.ds(p, 1)] = folded(x[pl.ds(p * BLOCK, BLOCK), :])

    def chunk(c):
        cells = y[pl.ds(c * 2 * BLOCK, 2 * BLOCK), :]
        dims = (((1,), (1,)), ((), ()))
        crossed = lax.dot_general(x[...], cells, dims, preferred_element_type=jnp.float32)
        crossed = crossed * (2.0 / (E * EPS))
        for half in range(2):
            norm = folded(cells[half * BLOCK : (half + 1) * BLOCK])
            spread[2 * c + half] = jnp.broadcast_to(-norm, (8, BLOCK))
            for p in range(SB):
                gram[p, 2 * c + half] = crossed[
                    p * BLOCK : (p + 1) * BLOCK, half * BLOCK : (half + 1) * BLOCK
                ]

    for c in range(TB // 2):
        chunk(c)
    y_start[...] = spread[...][:, 0]
    before = zeros[...] - x_norm[...]
    spread_rows(before + OFFSET, row_spread)
    live = fetched(lists, counts)
    row_pass(pairs, live, gram, spread, before, row_spread, sums, found, peaks, nothing)
    for d in range(SB):
        partial[d] = found[...]


def col_kernel(
    pairs_hbm,
    counts_hbm,
    gram,
    partials,
    mass_log,
    before,
    partial,
    potential,
    pairs,
    counts,
    done,
    spread,
    col_spread,
    peaks,
    sums,
    found,
):
    lists = fetch(pairs_hbm, counts_hbm, pairs, counts, done)
    potential[...] = mass_log[...] - log_sum(partials[...])
    spread_rows(potential[...], spread)
    spread_cols(before[...] + OFFSET, col_spread)
    sums[...] = jnp.zeros(sums.shape, jnp.float32)
    live = fetched(lists, counts)

    def scores(p, q):
        return (spread[p] + gram[p, q]).reshape(BLOCK // 8, 8, BLOCK)

    def only(slots):
        places = [entry(pairs, k) for k in slots]
        parts = [jnp.sum(jnp.exp(scores(p, q) + col_spread[q][None]), axis=0) for p, q in places]
        for (p, q), part in zip(places, parts):
            sums[q] += part

    each(live, COL_STEP, only)
    totals = jnp.sum(sums[...], axis=1)
    found[...] = jnp.log(totals) - (before[...] + OFFSET)

    @pl.when(jnp.logical_not(in_range(totals)))
    def again():
        peaks[...] = jnp.full(peaks.shape, -jnp.inf, jnp.float32)
        sums[...] = jnp.zeros(sums.shape, jnp.float32)

        def first(k, unused):
            p, q = entry(pairs, k)
            peaks[q] = jnp.maximum(peaks[q], jnp.max(scores(p, q), axis=0))
            return unused

        lax.fori_loop(0, live, first, 0)
        peaks[...] = jnp.broadcast_to(jnp.max(peaks[...], axis=1, keepdims=True), peaks.shape)

        def second(k, unused):
            p, q = entry(pairs, k)
            sums[q] += jnp.sum(jnp.exp(scores(p, q) - peaks[q][None]), axis=0)
            return unused

        lax.fori_loop(0, live, second, 0)
        found[...] = peaks[...][:, 0] + jnp.log(jnp.sum(sums[...], axis=1))

    for d in range(Z):
        partial[d] = found[...]


def merge_kernel(partials, merged):
    found = log_sum(partials[...])
    merged[...] = jnp.broadcast_to(found[None], merged.shape)


def row_kernel(
    pairs_hbm,
    counts_hbm,
    gram,
    partials,
    mass,
    before,
    partial,
    potential,
    pairs,
    counts,
    done,
    spread,
    row_spread,
    peaks,
    sums,
    found,
):
    lists = fetch(pairs_hbm, counts_hbm, pairs, counts, done)
    potential[...] = jnp.log(mass[...]) - log_sum(partials[...])
    spread_cols(potential[...], spread)
    spread_rows(before[...] + OFFSET, row_spread)
    live = fetched(lists, counts)
    row_pass(
        pairs, live, gram, spread, before[...], row_spread, sums, found, peaks, nothing
    )
    for d in range(SB):
        partial[d] = found[...]


def map_kernel(
    pairs_hbm,
    counts_hbm,
    gram,
    partials,
    mass,
    before,
    x_norm,
    y_start,
    y,
    packet,
    row_pot,
    col_pot,
    pairs,
    counts,
    done,
    spread,
    row_spread,
    peaks,
    sums,
    found,
    high,
    low,
    rows_out,
    cols_out,
):
    lists = fetch(pairs_hbm, counts_hbm, pairs, counts, done)
    potential = jnp.log(mass[...]) - log_sum(partials[...])
    rows_out[...] = EPS * (before[...] + x_norm[...])
    cols_out[...] = EPS * (potential - y_start[...])
    copies = [
        pltpu.make_async_copy(rows_out, row_pot, done.at[2]),
        pltpu.make_async_copy(cols_out, col_pot, done.at[3]),
    ]
    for copy in copies:
        copy.start()
    spread_cols(potential, spread)
    spread_rows(before[...] + OFFSET, row_spread)
    high[...] = jnp.zeros(high.shape, jnp.bfloat16)
    low[...] = jnp.zeros(low.shape, jnp.bfloat16)

    def also(p, q, weight):
        rows = pl.ds(pl.multiple_of(p * BLOCK, BLOCK), BLOCK)
        cols = pl.ds(pl.multiple_of(q * BLOCK, BLOCK), BLOCK)
        leading = weight.astype(jnp.bfloat16)
        high[rows, cols] = leading
        low[rows, cols] = (weight - leading.astype(jnp.float32)).astype(jnp.bfloat16)

    live = fetched(lists, counts)
    row_pass(pairs, live, gram, spread, before[...], row_spread, sums, found, peaks, also)
    total = jnp.dot(high[...], y[...], preferred_element_type=jnp.float32) + jnp.dot(
        low[...], y[...], preferred_element_type=jnp.float32
    )
    for p in range(SB):
        packet[p, pl.ds(0, BLOCK), :] = total[p * BLOCK : (p + 1) * BLOCK] / jnp.sum(
            sums[p], axis=1, keepdims=True
        )
        packet[p, pl.ds(BLOCK, 8), :] = jnp.concatenate(
            [jnp.broadcast_to(found[pl.ds(p, 1)], (8, BLOCK))] * 2, axis=1
        )
    for copy in copies:
        copy.wait()


def mix_kernel(packets, mapped):
    parts = jnp.concatenate([packets[t, pl.ds(BLOCK, 1), pl.ds(0, BLOCK)] for t in range(SB)])
    share = jnp.exp(parts - jnp.max(parts, axis=0, keepdims=True))
    share = share / jnp.sum(share, axis=0, keepdims=True)
    total = jnp.zeros((BLOCK, E), jnp.float32)
    for t in range(SB):
        factor = turned(jnp.broadcast_to(share[t : t + 1], (BLOCK, BLOCK)))
        total = total + jnp.concatenate([factor, factor], axis=1) * packets[t, pl.ds(0, BLOCK), :]
    mapped[...] = jnp.broadcast_to(total[None], mapped.shape)


def shards(source_cells, target_cells, source_mass, target_mass, pairs, counts):
    pairs = pairs.reshape(MAXB)
    counts = counts.reshape(1)
    source_mass = source_mass.reshape(SB, BLOCK)
    target_mass = target_mass.reshape(TB, BLOCK)
    tall = pltpu.VMEM((SB, BLOCK, BLOCK), jnp.float32)
    flat = pltpu.VMEM((TB, 8, BLOCK), jnp.float32)
    rows = pltpu.VMEM((SB, BLOCK), jnp.float32)
    cols = pltpu.VMEM((TB, BLOCK), jnp.float32)
    dense = pltpu.VMEM((SB * BLOCK, TB * BLOCK), jnp.bfloat16)
    lists = [pltpu.SMEM((MAXB,), jnp.int32), pltpu.SMEM((1,), jnp.int32)]

    def sems(count):
        return pltpu.SemaphoreType.DMA((count,))

    zeros = call(zero_kernel, f32(SB, BLOCK), [], "zeros", [], flops=FIRST)()
    gram, row_part, x_norm, y_start, source_log = call(
        gram_kernel,
        (
            f32(SB, TB, BLOCK, BLOCK),
            f32(SB, SB, BLOCK),
            f32(SB, BLOCK),
            f32(TB, BLOCK),
            f32(SB, BLOCK),
        ),
        lists + [sems(2), flat, tall, tall, tall, rows],
        "gram",
        [ANY] * 2 + [VMEM] * 4,
    )(pairs, counts, source_cells, target_cells, source_mass, zeros)
    col_pot = y_start
    for iteration in range(ITERS):
        row_parts = lax.all_to_all(row_part, "t", 0, 0)
        col_part, row_pot = call(
            col_kernel,
            (f32(Z, TB, BLOCK), f32(SB, BLOCK)),
            lists + [sems(2), tall, flat, flat, flat, cols],
            "cols",
            [ANY] * 2 + [VMEM] * 4,
        )(pairs, counts, gram, row_parts, source_log, col_pot)
        col_parts = lax.all_to_all(col_part, "z", 0, 0)
        col_parts = call(merge_kernel, f32(XC, TB, BLOCK), [], "merge", [VMEM])(col_parts)
        col_parts = lax.all_to_all(col_parts, ("x", "c"), 0, 0)
        if iteration < ITERS - 1:
            row_part, col_pot = call(
                row_kernel,
                (f32(SB, SB, BLOCK), f32(TB, BLOCK)),
                lists + [sems(2), flat, tall, tall, tall, rows],
                "rows",
                [ANY] * 2 + [VMEM] * 4,
            )(pairs, counts, gram, col_parts, target_mass, row_pot)
    packet, row_pot, col_pot = call(
        map_kernel,
        (f32(SB, BLOCK + 8, E), f32(SB, BLOCK), f32(TB, BLOCK)),
        lists + [sems(4), flat, tall, tall, tall, rows, dense, dense, rows, cols],
        "mapping",
        [ANY] * 2 + [VMEM] * 7,
        out_specs=(VMEM, ANY, ANY),
    )(pairs, counts, gram, col_parts, target_mass, row_pot, x_norm, y_start, target_cells)
    packets = lax.all_to_all(packet, "t", 0, 0)
    quarters = call(mix_kernel, f32(SB, BLOCK, E), [], "mix", [VMEM])(packets)
    mapped = lax.all_to_all(quarters, "t", 0, 0)
    return row_pot.reshape(-1), col_pot.reshape(-1), mapped.reshape(SB * BLOCK, E)


def solution(mesh):
    fine = Mesh(mesh.devices.reshape(Z, 4, 2, 4), ("z", "x", "c", "t"))
    return jax.shard_map(
        shards,
        mesh=fine,
        in_specs=(P(SRC, None), P("t", None), P(SRC), P("t"), P(SRC, "t", None), P(SRC, "t")),
        out_specs=(P(SRC), P("t"), P(SRC, None)),
        check_vma=False,
    )
```

```python
import jax
import jax.numpy as jnp
from jax import lax
from jax.experimental import pallas as pl
from jax.experimental.pallas import tpu as pltpu
from jax.sharding import Mesh
from jax.sharding import PartitionSpec as P

BLOCK = 128
ITERS = 3
SB = 4
TB = 16
MAXB = 32
E = 256
XC = 8
Z = 16
EPS = 0.02
SRC = ("z", "x", "c")


VMEM = pl.BlockSpec(memory_space=pltpu.VMEM)
ANY = pl.BlockSpec(memory_space=pl.ANY)
OFFSET = 70.0
FIRST = 5000000000
ROW_STEP = 4
COL_STEP = 4
MIDDLE = 10.0
REACH = 74.0
FIRST_LIMIT = 52


def call(kernel, out_shape, scratch, name, specs, out_specs=None, flops=1000000):
    return pl.pallas_call(
        kernel,
        out_shape=out_shape,
        in_specs=specs,
        out_specs=out_specs or jax.tree.map(lambda unused: VMEM, out_shape),
        scratch_shapes=scratch,
        compiler_params=pltpu.CompilerParams(vmem_limit_bytes=16 * 1024 * 1024),
        cost_estimate=pl.CostEstimate(flops=flops, bytes_accessed=2000000, transcendentals=500000),
        name=name,
    )


def f32(*shape):
    return jax.ShapeDtypeStruct(shape, jnp.float32)


def fetch(listed, pairs):
    for k in range(MAXB):
        pairs[k] = listed[0, k]
    return listed[1, 0]


def each(live, step, body):
    whole = live >> (step.bit_length() - 1)

    def several(i, unused):
        body([i * step + j for j in range(step)])
        return unused

    def single(k, unused):
        body([k])
        return unused

    lax.fori_loop(0, whole, several, 0)
    lax.fori_loop(whole * step, live, single, 0)


def entry(pairs, k):
    value = pairs[k]
    return value >> 4, value & 15


def turned(block):
    return jnp.transpose(block, (1, 0))


def log_sum(parts):
    top = jnp.max(parts, axis=0)
    return top + jnp.log(jnp.sum(jnp.exp(parts - top[None]), axis=0))


def in_range(logs):
    return jnp.max(jnp.abs(logs - MIDDLE)) <= REACH


def spread_rows(potential, spread):
    for p in range(SB):
        spread[p] = turned(jnp.broadcast_to(potential[p : p + 1], (BLOCK, BLOCK)))


def spread_cols(potential, spread):
    for q in range(TB):
        spread[q] = jnp.broadcast_to(potential[q : q + 1], (8, BLOCK))


def row_scores(gram, spread, p, q):
    score = spread[q][None] + gram[p, q].reshape(BLOCK // 8, 8, BLOCK)
    return score.reshape(BLOCK, BLOCK)


def row_totals(sums):
    return jnp.concatenate(
        [jnp.sum(turned(sums[p]), axis=0, keepdims=True) for p in range(SB)], axis=0
    )


def row_passes(pairs, live, gram, spread, peaks, sums, found, also):
    peaks[...] = jnp.full(peaks.shape, -jnp.inf, jnp.float32)
    sums[...] = jnp.zeros(sums.shape, jnp.float32)

    def first(k, unused):
        p, q = entry(pairs, k)
        peaks[p] = jnp.maximum(peaks[p], row_scores(gram, spread, p, q))
        return unused

    lax.fori_loop(0, live, first, 0)
    for p in range(SB):
        peaks[p] = jnp.broadcast_to(jnp.max(peaks[p], axis=1, keepdims=True), (BLOCK, BLOCK))

    def second(k, unused):
        p, q = entry(pairs, k)
        weight = jnp.exp(row_scores(gram, spread, p, q) - peaks[p])
        sums[p] += weight
        also(p, q, weight)
        return unused

    lax.fori_loop(0, live, second, 0)
    tops = jnp.concatenate([turned(peaks[p])[0:1] for p in range(SB)], axis=0)
    found[...] = tops + jnp.log(row_totals(sums))


def row_pass(pairs, live, gram, spread, before, row_spread, sums, found, peaks, also):
    sums[...] = jnp.zeros(sums.shape, jnp.float32)

    def only(slots):
        places = [entry(pairs, k) for k in slots]
        weights = [jnp.exp(row_scores(gram, spread, p, q) + row_spread[p]) for p, q in places]
        for (p, q), weight in zip(places, weights):
            sums[p] += weight
            also(p, q, weight)

    each(live, ROW_STEP, only)
    logs = jnp.log(row_totals(sums))
    found[...] = logs - (before + OFFSET)

    @pl.when(jnp.logical_not(in_range(logs)))
    def again():
        row_passes(pairs, live, gram, spread, peaks, sums, found, also)


def folded(cells):
    wide = cells.astype(jnp.float32)
    square = wide * wide
    square = turned(square[:, :BLOCK] + square[:, BLOCK:])
    return jnp.sum(square, axis=0, keepdims=True) * (1.0 / (E * EPS))


def nothing(p, q, weight):
    return None


def zero_kernel(zeros):
    zeros[...] = jnp.zeros(zeros.shape, jnp.float32)


def gram_kernel(
    pairs_in,
    counts,
    x,
    y,
    mass,
    zeros,
    gram,
    partial,
    x_norm,
    y_start,
    log_mass,
    listed,
    pairs,
    spread,
    row_spread,
    peaks,
    sums,
    found,
):
    listed[...] = jnp.zeros(listed.shape, jnp.int32)
    listed[pl.ds(0, 1), pl.ds(0, MAXB)] = pairs_in[...]
    listed[pl.ds(1, 1), pl.ds(0, 1)] = counts[...]
    log_mass[...] = jnp.log(mass[...])
    for p in range(SB):
        x_norm[pl.ds(p, 1)] = folded(x[pl.ds(p * BLOCK, BLOCK), :])

    def chunk(c):
        cells = y[pl.ds(c * 2 * BLOCK, 2 * BLOCK), :]
        dims = (((1,), (1,)), ((), ()))
        crossed = lax.dot_general(x[...], cells, dims, preferred_element_type=jnp.float32)
        crossed = crossed * (2.0 / (E * EPS))
        for half in range(2):
            norm = folded(cells[half * BLOCK : (half + 1) * BLOCK])
            spread[2 * c + half] = jnp.broadcast_to(-norm, (8, BLOCK))
            for p in range(SB):
                gram[p, 2 * c + half] = crossed[
                    p * BLOCK : (p + 1) * BLOCK, half * BLOCK : (half + 1) * BLOCK
                ]

    for c in range(TB // 2):
        chunk(c)
    y_start[...] = spread[...][:, 0]
    before = zeros[...] - x_norm[...]
    spread_rows(before + OFFSET, row_spread)
    live = fetch(listed, pairs)
    row_pass(pairs, live, gram, spread, before, row_spread, sums, found, peaks, nothing)
    for d in range(SB):
        partial[d] = found[...]


def col_kernel(
    listed,
    gram,
    partials,
    mass_log,
    before,
    partial,
    potential,
    pairs,
    spread,
    col_spread,
    peaks,
    sums,
    found,
):
    potential[...] = mass_log[...] - log_sum(partials[...])
    spread_rows(potential[...], spread)
    spread_cols(before[...] + OFFSET, col_spread)
    sums[...] = jnp.zeros(sums.shape, jnp.float32)
    live = fetch(listed, pairs)

    def scores(p, q):
        return (spread[p] + gram[p, q]).reshape(BLOCK // 8, 8, BLOCK)

    def only(slots):
        places = [entry(pairs, k) for k in slots]
        parts = [jnp.sum(jnp.exp(scores(p, q) + col_spread[q][None]), axis=0) for p, q in places]
        for (p, q), part in zip(places, parts):
            sums[q] += part

    each(live, COL_STEP, only)
    logs = jnp.log(jnp.sum(sums[...], axis=1))
    found[...] = logs - (before[...] + OFFSET)

    @pl.when(jnp.logical_not(in_range(logs)))
    def again():
        peaks[...] = jnp.full(peaks.shape, -jnp.inf, jnp.float32)
        sums[...] = jnp.zeros(sums.shape, jnp.float32)

        def first(k, unused):
            p, q = entry(pairs, k)
            peaks[q] = jnp.maximum(peaks[q], jnp.max(scores(p, q), axis=0))
            return unused

        lax.fori_loop(0, live, first, 0)
        peaks[...] = jnp.broadcast_to(jnp.max(peaks[...], axis=1, keepdims=True), peaks.shape)

        def second(k, unused):
            p, q = entry(pairs, k)
            sums[q] += jnp.sum(jnp.exp(scores(p, q) - peaks[q][None]), axis=0)
            return unused

        lax.fori_loop(0, live, second, 0)
        found[...] = peaks[...][:, 0] + jnp.log(jnp.sum(sums[...], axis=1))

    for d in range(Z):
        partial[d] = found[...]


def merge_kernel(partials, merged):
    found = log_sum(partials[...])
    merged[...] = jnp.broadcast_to(found[None], merged.shape)


def row_kernel(
    listed,
    gram,
    partials,
    mass,
    before,
    partial,
    potential,
    pairs,
    spread,
    row_spread,
    peaks,
    sums,
    found,
):
    potential[...] = jnp.log(mass[...]) - log_sum(partials[...])
    spread_cols(potential[...], spread)
    spread_rows(before[...] + OFFSET, row_spread)
    live = fetch(listed, pairs)
    row_pass(
        pairs, live, gram, spread, before[...], row_spread, sums, found, peaks, nothing
    )
    for d in range(SB):
        partial[d] = found[...]


def map_kernel(
    listed,
    gram,
    partials,
    mass,
    before,
    x_norm,
    y_start,
    y,
    packet,
    row_pot,
    col_pot,
    pairs,
    done,
    spread,
    row_spread,
    peaks,
    sums,
    found,
    high,
    low,
    rows_out,
    cols_out,
):
    potential = jnp.log(mass[...]) - log_sum(partials[...])
    rows_out[...] = EPS * (before[...] + x_norm[...])
    cols_out[...] = EPS * (potential - y_start[...])
    copies = [
        pltpu.make_async_copy(rows_out, row_pot, done.at[0]),
        pltpu.make_async_copy(cols_out, col_pot, done.at[1]),
    ]
    for copy in copies:
        copy.start()
    spread_cols(potential, spread)
    spread_rows(before[...] + OFFSET, row_spread)
    high[...] = jnp.zeros(high.shape, jnp.bfloat16)
    low[...] = jnp.zeros(low.shape, jnp.bfloat16)

    def also(p, q, weight):
        rows = pl.ds(pl.multiple_of(p * BLOCK, BLOCK), BLOCK)
        cols = pl.ds(pl.multiple_of(q * BLOCK, BLOCK), BLOCK)
        leading = weight.astype(jnp.bfloat16)
        high[rows, cols] = leading
        low[rows, cols] = (weight - leading.astype(jnp.float32)).astype(jnp.bfloat16)

    live = fetch(listed, pairs)
    row_pass(pairs, live, gram, spread, before[...], row_spread, sums, found, peaks, also)
    total = jnp.dot(high[...], y[...], preferred_element_type=jnp.float32) + jnp.dot(
        low[...], y[...], preferred_element_type=jnp.float32
    )
    for p in range(SB):
        packet[p, pl.ds(0, BLOCK), :] = total[p * BLOCK : (p + 1) * BLOCK] / jnp.sum(
            sums[p], axis=1, keepdims=True
        )
        packet[p, pl.ds(BLOCK, 8), :] = jnp.concatenate(
            [jnp.broadcast_to(found[pl.ds(p, 1)], (8, BLOCK))] * 2, axis=1
        )
    for copy in copies:
        copy.wait()


def mix_kernel(packets, mapped):
    parts = jnp.concatenate([packets[t, pl.ds(BLOCK, 1), pl.ds(0, BLOCK)] for t in range(SB)])
    share = jnp.exp(parts - jnp.max(parts, axis=0, keepdims=True))
    share = share / jnp.sum(share, axis=0, keepdims=True)
    total = jnp.zeros((BLOCK, E), jnp.float32)
    for t in range(SB):
        factor = turned(jnp.broadcast_to(share[t : t + 1], (BLOCK, BLOCK)))
        total = total + jnp.concatenate([factor, factor], axis=1) * packets[t, pl.ds(0, BLOCK), :]
    mapped[...] = jnp.broadcast_to(total[None], mapped.shape)


def shards(source_cells, target_cells, source_mass, target_mass, pairs, counts):
    pairs = pairs.reshape(1, MAXB)
    counts = counts.reshape(1, 1)
    source_mass = source_mass.reshape(SB, BLOCK)
    target_mass = target_mass.reshape(TB, BLOCK)
    tall = pltpu.VMEM((SB, BLOCK, BLOCK), jnp.float32)
    flat = pltpu.VMEM((TB, 8, BLOCK), jnp.float32)
    rows = pltpu.VMEM((SB, BLOCK), jnp.float32)
    cols = pltpu.VMEM((TB, BLOCK), jnp.float32)
    dense = pltpu.VMEM((SB * BLOCK, TB * BLOCK), jnp.bfloat16)
    lists = [pltpu.SMEM((MAXB,), jnp.int32)]

    def sems(count):
        return pltpu.SemaphoreType.DMA((count,))

    zeros = call(zero_kernel, f32(SB, BLOCK), [], "zeros", [], flops=FIRST)()
    gram, row_part, x_norm, y_start, source_log, listed = call(
        gram_kernel,
        (
            f32(SB, TB, BLOCK, BLOCK),
            f32(SB, SB, BLOCK),
            f32(SB, BLOCK),
            f32(TB, BLOCK),
            f32(SB, BLOCK),
            jax.ShapeDtypeStruct((8, BLOCK), jnp.int32),
        ),
        lists + [flat, tall, tall, tall, rows],
        "gram",
        [VMEM] * 6,
    )(pairs, counts, source_cells, target_cells, source_mass, zeros)
    col_pot = y_start
    for iteration in range(ITERS):
        row_parts = lax.all_to_all(row_part, "t", 0, 0)
        col_part, row_pot = call(
            col_kernel,
            (f32(Z, TB, BLOCK), f32(SB, BLOCK)),
            lists + [tall, flat, flat, flat, cols],
            "cols",
            [VMEM] + [VMEM] * 4,
        )(listed, gram, row_parts, source_log, col_pot)
        col_parts = lax.all_to_all(col_part, "z", 0, 0)
        col_parts = call(merge_kernel, f32(XC, TB, BLOCK), [], "merge", [VMEM])(col_parts)
        col_parts = lax.all_to_all(col_parts, ("x", "c"), 0, 0)
        if iteration < ITERS - 1:
            row_part, col_pot = call(
                row_kernel,
                (f32(SB, SB, BLOCK), f32(TB, BLOCK)),
                lists + [flat, tall, tall, tall, rows],
                "rows",
                [VMEM] + [VMEM] * 4,
            )(listed, gram, col_parts, target_mass, row_pot)
    packet, row_pot, col_pot = call(
        map_kernel,
        (f32(SB, BLOCK + 8, E), f32(SB, BLOCK), f32(TB, BLOCK)),
        lists + [sems(2), flat, tall, tall, tall, rows, dense, dense, rows, cols],
        "mapping",
        [VMEM] + [VMEM] * 7,
        out_specs=(VMEM, ANY, ANY),
    )(listed, gram, col_parts, target_mass, row_pot, x_norm, y_start, target_cells)
    packets = lax.all_to_all(packet, "t", 0, 0)
    quarters = call(mix_kernel, f32(SB, BLOCK, E), [], "mix", [VMEM])(packets)
    mapped = lax.all_to_all(quarters, "t", 0, 0)
    return row_pot.reshape(-1), col_pot.reshape(-1), mapped.reshape(SB * BLOCK, E)


def solution(mesh):
    fine = Mesh(mesh.devices.reshape(Z, 4, 2, 4), ("z", "x", "c", "t"))
    return jax.shard_map(
        shards,
        mesh=fine,
        in_specs=(P(SRC, None), P("t", None), P(SRC), P("t"), P(SRC, "t", None), P(SRC, "t")),
        out_specs=(P(SRC), P("t"), P(SRC, None)),
        check_vma=False,
    )
```

```python
import jax
import jax.numpy as jnp
from jax import lax
from jax.experimental import pallas as pl
from jax.experimental.pallas import tpu as pltpu
from jax.sharding import Mesh
from jax.sharding import PartitionSpec as P

BLOCK = 128
ITERS = 3
SB = 4
TB = 16
MAXB = 32
E = 256
XC = 8
Z = 16
LISTS = TB * BLOCK
MASS = LISTS + 8
HEIGHT = MASS + TB
EPS = 0.02
SRC = ("z", "x", "c")


VMEM = pl.BlockSpec(memory_space=pltpu.VMEM)
ANY = pl.BlockSpec(memory_space=pl.ANY)
OFFSET = 70.0
LIMIT = 51
FIRST = 5000000000
ROW_STEP = 4
COL_STEP = 4
MIDDLE = 10.0
REACH = 74.0
FIRST_LIMIT = 52


def call(kernel, out_shape, scratch, name, specs, out_specs=None, flops=1000000, limit=16):
    return pl.pallas_call(
        kernel,
        out_shape=out_shape,
        in_specs=specs,
        out_specs=out_specs or jax.tree.map(lambda unused: VMEM, out_shape),
        scratch_shapes=scratch,
        compiler_params=pltpu.CompilerParams(vmem_limit_bytes=limit * 1024 * 1024),
        cost_estimate=pl.CostEstimate(flops=flops, bytes_accessed=2000000, transcendentals=500000),
        name=name,
    )


def f32(*shape):
    return jax.ShapeDtypeStruct(shape, jnp.float32)


def fetch(listed, pairs):
    for k in range(MAXB):
        pairs[k] = listed[0, k]
    return listed[1, 0]


def each(live, step, body):
    whole = live >> (step.bit_length() - 1)

    def several(i, unused):
        body([i * step + j for j in range(step)])
        return unused

    def single(k, unused):
        body([k])
        return unused

    lax.fori_loop(0, whole, several, 0)
    lax.fori_loop(whole * step, live, single, 0)


def entry(pairs, k):
    value = pairs[k]
    return value >> 4, value & 15


def turned(block):
    return jnp.transpose(block, (1, 0))


def log_sum(parts):
    top = jnp.max(parts, axis=0)
    return top + jnp.log(jnp.sum(jnp.exp(parts - top[None]), axis=0))


def in_range(logs):
    return jnp.max(jnp.abs(logs - MIDDLE)) <= REACH


def spread_rows(potential, spread):
    for p in range(SB):
        spread[p] = turned(jnp.broadcast_to(potential[p : p + 1], (BLOCK, BLOCK)))


def spread_cols(potential, spread):
    for q in range(TB):
        spread[q] = jnp.broadcast_to(potential[q : q + 1], (8, BLOCK))


def row_scores(gram, spread, p, q):
    score = spread[q][None] + gram[p, q].reshape(BLOCK // 8, 8, BLOCK)
    return score.reshape(BLOCK, BLOCK)


def row_totals(sums):
    return jnp.concatenate(
        [jnp.sum(turned(sums[p]), axis=0, keepdims=True) for p in range(SB)], axis=0
    )


def row_passes(pairs, live, gram, spread, peaks, sums, found):
    peaks[...] = jnp.full(peaks.shape, -jnp.inf, jnp.float32)
    sums[...] = jnp.zeros(sums.shape, jnp.float32)

    def first(k, unused):
        p, q = entry(pairs, k)
        peaks[p] = jnp.maximum(peaks[p], row_scores(gram, spread, p, q))
        return unused

    lax.fori_loop(0, live, first, 0)
    for p in range(SB):
        peaks[p] = jnp.broadcast_to(jnp.max(peaks[p], axis=1, keepdims=True), (BLOCK, BLOCK))

    def second(k, unused):
        p, q = entry(pairs, k)
        weight = jnp.exp(row_scores(gram, spread, p, q) - peaks[p])
        sums[p] += weight
        return unused

    lax.fori_loop(0, live, second, 0)
    tops = jnp.concatenate([turned(peaks[p])[0:1] for p in range(SB)], axis=0)
    found[...] = tops + jnp.log(row_totals(sums))


def row_pass(pairs, live, gram, spread, before, row_spread, sums, found, peaks):
    sums[...] = jnp.zeros(sums.shape, jnp.float32)

    def only(slots):
        places = [entry(pairs, k) for k in slots]
        weights = [jnp.exp(row_scores(gram, spread, p, q) + row_spread[p]) for p, q in places]
        for (p, q), weight in zip(places, weights):
            sums[p] += weight

    each(live, ROW_STEP, only)
    logs = jnp.log(row_totals(sums))
    found[...] = logs - (before + OFFSET)

    @pl.when(jnp.logical_not(in_range(logs)))
    def again():
        row_passes(pairs, live, gram, spread, peaks, sums, found)


def folded(cells):
    wide = cells.astype(jnp.float32)
    square = wide * wide
    square = turned(square[:, :BLOCK] + square[:, BLOCK:])
    return jnp.sum(square, axis=0, keepdims=True) * (1.0 / (E * EPS))


def multiplied(x, cells, c, gram):
    dims = (((1,), (1,)), ((), ()))
    crossed = lax.dot_general(x[...], cells, dims, preferred_element_type=jnp.float32)
    crossed = crossed * (2.0 / (E * EPS))
    for half in range(2):
        for p in range(SB):
            gram[p, 2 * c + half] = crossed[
                p * BLOCK : (p + 1) * BLOCK, half * BLOCK : (half + 1) * BLOCK
            ]


def zero_kernel(zeros):
    zeros[...] = jnp.zeros(zeros.shape, jnp.float32)


def gram_kernel(
    pairs_in,
    counts,
    x,
    y,
    mass,
    y_mass,
    zeros,
    gram,
    partial,
    x_norm,
    y_start,
    log_mass,
    listed,
    wide_hbm,
    pairs,
    wide,
    done,
    spread,
    row_spread,
    peaks,
    sums,
    found,
):
    listed[...] = jnp.zeros(listed.shape, jnp.int32)
    listed[pl.ds(0, 1), pl.ds(0, MAXB)] = pairs_in[...]
    listed[pl.ds(1, 1), pl.ds(0, 1)] = counts[...]
    log_mass[...] = jnp.log(mass[...])
    wide[pl.ds(LISTS, 8)] = jnp.zeros((8, E), jnp.float32)
    wide[pl.ds(LISTS, 8), pl.ds(0, BLOCK)] = listed[...].astype(jnp.float32)
    wide[pl.ds(MASS, TB)] = jnp.zeros((TB, E), jnp.float32)
    wide[pl.ds(MASS, TB), pl.ds(0, BLOCK)] = y_mass[...]
    copies = []

    def send(start, size):
        span = pl.ds(start, size)
        copies.append(
            pltpu.make_async_copy(wide.at[span], wide_hbm.at[span], done.at[len(copies)])
        )
        copies[-1].start()

    send(LISTS, 8 + TB)
    for c in range(TB // 4):
        span = pl.ds(c * 4 * BLOCK, 4 * BLOCK)
        wide[span] = y[span].astype(jnp.float32)
        send(c * 4 * BLOCK, 4 * BLOCK)
    for p in range(SB):
        x_norm[pl.ds(p, 1)] = folded(x[pl.ds(p * BLOCK, BLOCK), :])

    for c in range(TB // 2):
        cells = y[pl.ds(c * 2 * BLOCK, 2 * BLOCK), :]
        multiplied(x, cells, c, gram)
        for half in range(2):
            norm = folded(cells[half * BLOCK : (half + 1) * BLOCK])
            spread[2 * c + half] = jnp.broadcast_to(-norm, (8, BLOCK))
    y_start[...] = spread[...][:, 0]
    before = zeros[...] - x_norm[...]
    spread_rows(before + OFFSET, row_spread)
    live = fetch(listed, pairs)
    row_pass(pairs, live, gram, spread, before, row_spread, sums, found, peaks)
    for d in range(SB):
        partial[d] = found[...]
    for copy in copies:
        copy.wait()


def col_kernel(
    listed,
    gram,
    partials,
    mass_log,
    before,
    partial,
    potential,
    pairs,
    spread,
    col_spread,
    peaks,
    sums,
    found,
):
    potential[...] = mass_log[...] - log_sum(partials[...])
    spread_rows(potential[...], spread)
    spread_cols(before[...] + OFFSET, col_spread)
    sums[...] = jnp.zeros(sums.shape, jnp.float32)
    live = fetch(listed, pairs)

    def scores(p, q):
        return (spread[p] + gram[p, q]).reshape(BLOCK // 8, 8, BLOCK)

    def only(slots):
        places = [entry(pairs, k) for k in slots]
        parts = [jnp.sum(jnp.exp(scores(p, q) + col_spread[q][None]), axis=0) for p, q in places]
        for (p, q), part in zip(places, parts):
            sums[q] += part

    each(live, COL_STEP, only)
    logs = jnp.log(jnp.sum(sums[...], axis=1))
    found[...] = logs - (before[...] + OFFSET)

    @pl.when(jnp.logical_not(in_range(logs)))
    def again():
        peaks[...] = jnp.full(peaks.shape, -jnp.inf, jnp.float32)
        sums[...] = jnp.zeros(sums.shape, jnp.float32)

        def first(k, unused):
            p, q = entry(pairs, k)
            peaks[q] = jnp.maximum(peaks[q], jnp.max(scores(p, q), axis=0))
            return unused

        lax.fori_loop(0, live, first, 0)
        peaks[...] = jnp.broadcast_to(jnp.max(peaks[...], axis=1, keepdims=True), peaks.shape)

        def second(k, unused):
            p, q = entry(pairs, k)
            sums[q] += jnp.sum(jnp.exp(scores(p, q) - peaks[q][None]), axis=0)
            return unused

        lax.fori_loop(0, live, second, 0)
        found[...] = peaks[...][:, 0] + jnp.log(jnp.sum(sums[...], axis=1))

    for d in range(Z):
        partial[d] = found[...]


def merge_kernel(partials, merged):
    found = log_sum(partials[...])
    merged[...] = jnp.broadcast_to(found[None], merged.shape)


def row_kernel(
    listed,
    gram,
    partials,
    mass,
    before,
    partial,
    potential,
    pairs,
    spread,
    row_spread,
    peaks,
    sums,
    found,
):
    potential[...] = jnp.log(mass[...]) - log_sum(partials[...])
    spread_cols(potential[...], spread)
    spread_rows(before[...] + OFFSET, row_spread)
    live = fetch(listed, pairs)
    row_pass(
        pairs, live, gram, spread, before[...], row_spread, sums, found, peaks
    )
    for d in range(SB):
        partial[d] = found[...]


def map_kernel(
    listed,
    partials,
    mass,
    before,
    x_norm,
    y_start,
    x,
    y,
    wide_hbm,
    row_pot,
    col_pot,
    mapped,
    mask,
    done,
    wide,
    cells,
    weights,
    lists,
    lse,
    spread,
    row_spread,
    peaks,
    sums,
    total,
    rows_out,
    cols_out,
):
    own = lax.axis_index("t")

    def shard_of(i):
        return (own + i) & (SB - 1)

    def arrival(i):
        rows = pl.ds(pl.multiple_of(shard_of(i) * HEIGHT, 8), HEIGHT)
        return pltpu.make_async_copy(wide_hbm.at[rows], wide.at[i - 1], done.at[i - 1])

    for i in range(1, SB):
        arrival(i).start()
    for t in range(SB):
        lse[t] = log_sum(jnp.stack([partials[SB * k + t] for k in range(XC)]))
    potential = jnp.log(mass[...]) - lse[own]
    rows_out[...] = EPS * (before[...] + x_norm[...])
    cols_out[...] = EPS * (potential - y_start[...])
    copies = [
        pltpu.make_async_copy(rows_out, row_pot, done.at[SB - 1]),
        pltpu.make_async_copy(cols_out, col_pot, done.at[SB]),
    ]
    for copy in copies:
        copy.start()
    spread_rows(before[...] + OFFSET, row_spread)

    def couple(found):
        for k in range(SB * TB):
            mask[k] = -jnp.inf
        live = found[1, 0]
        for k in range(MAXB):
            mask[jnp.where(k < live, found[0, k], SB * TB)] = 0.0

    def sweep(chunk_of, use):
        dims = (((1,), (1,)), ((), ()))
        for c in range(TB // 2):
            crossed = lax.dot_general(x[...], chunk_of(c), dims, preferred_element_type=jnp.float32)
            crossed = crossed * (2.0 / (E * EPS))
            for p in range(SB):
                for half in range(2):
                    q = 2 * c + half
                    part = crossed[p * BLOCK : (p + 1) * BLOCK, half * BLOCK : (half + 1) * BLOCK]
                    part = part.reshape(BLOCK // 8, 8, BLOCK) + (spread[q] + mask[p * TB + q])[None]
                    use(p, q, part.reshape(BLOCK, BLOCK))

    def weigh(p, q, score):
        weight = jnp.exp(score + row_spread[p]).astype(jnp.bfloat16)
        weights[pl.ds(p * BLOCK, BLOCK), pl.ds(q * BLOCK, BLOCK)] = weight
        sums[p] += weight.astype(jnp.float32)

    def top(p, q, score):
        peaks[p] = jnp.maximum(peaks[p], score)

    def load_own():
        spread_cols(jnp.log(mass[...]) - lse[own], spread)
        couple(listed)

    def own_chunk(c):
        return y[pl.ds(c * 2 * BLOCK, 2 * BLOCK)]

    def load(i):
        other = wide.at[i - 1]
        found = other[pl.ds(MASS, TB), pl.ds(0, BLOCK)]
        spread_cols(jnp.log(found) - lse[shard_of(i)], spread)
        lists[...] = other[pl.ds(LISTS, 8), pl.ds(0, BLOCK)].astype(jnp.int32)
        couple(lists)

    def chunk(i):
        def of(c):
            part = pl.ds(c * 2 * BLOCK, 2 * BLOCK)
            narrow = wide[i - 1, part, :].astype(jnp.bfloat16)
            cells[part] = narrow
            return narrow

        return of

    def weigh_all(arrived):
        sums[...] = jnp.zeros(sums.shape, jnp.float32)
        load_own()
        sweep(own_chunk, weigh)
        total[...] = jnp.dot(weights[...], y[...], preferred_element_type=jnp.float32)

        def other(i, unused):
            if not arrived:
                arrival(i).wait()
            load(i)
            sweep(chunk(i), weigh)
            total[...] += jnp.dot(weights[...], cells[...], preferred_element_type=jnp.float32)
            return unused

        lax.fori_loop(1, SB, other, 0)

    weigh_all(False)

    @pl.when(jnp.logical_not(in_range(jnp.log(row_totals(sums)))))
    def again():
        peaks[...] = jnp.full(peaks.shape, -jnp.inf, jnp.float32)
        load_own()
        sweep(own_chunk, top)

        def other(i, unused):
            load(i)
            sweep(chunk(i), top)
            return unused

        lax.fori_loop(1, SB, other, 0)
        for p in range(SB):
            highest = jnp.max(peaks[p], axis=1, keepdims=True)
            row_spread[p] = jnp.broadcast_to(-highest, (BLOCK, BLOCK))
        weigh_all(True)

    for p in range(SB):
        rows = pl.ds(p * BLOCK, BLOCK)
        total[rows] = total[rows] / jnp.sum(sums[p], axis=1, keepdims=True)
        copies.append(pltpu.make_async_copy(total.at[rows], mapped.at[rows], done.at[SB + 1 + p]))
        copies[-1].start()
    for copy in copies:
        copy.wait()


def shards(source_cells, target_cells, source_mass, target_mass, pairs, counts):
    pairs = pairs.reshape(1, MAXB)
    counts = counts.reshape(1, 1)
    source_mass = source_mass.reshape(SB, BLOCK)
    target_mass = target_mass.reshape(TB, BLOCK)
    tall = pltpu.VMEM((SB, BLOCK, BLOCK), jnp.float32)
    flat = pltpu.VMEM((TB, 8, BLOCK), jnp.float32)
    rows = pltpu.VMEM((SB, BLOCK), jnp.float32)
    cols = pltpu.VMEM((TB, BLOCK), jnp.float32)
    lists = [pltpu.SMEM((MAXB,), jnp.int32)]

    def sems(count):
        return pltpu.SemaphoreType.DMA((count,))

    zeros = call(zero_kernel, f32(SB, BLOCK), [], "zeros", [], flops=FIRST)()
    gram, row_part, x_norm, y_start, source_log, listed, wide = call(
        gram_kernel,
        (
            f32(SB, TB, BLOCK, BLOCK),
            f32(SB, SB, BLOCK),
            f32(SB, BLOCK),
            f32(TB, BLOCK),
            f32(SB, BLOCK),
            jax.ShapeDtypeStruct((8, BLOCK), jnp.int32),
            f32(HEIGHT, E),
        ),
        lists
        + [pltpu.VMEM((HEIGHT, E), jnp.float32), sems(TB // 4 + 1), flat, tall, tall, tall, rows],
        "gram",
        [VMEM] * 7,
        out_specs=(VMEM,) * 6 + (ANY,),
    )(pairs, counts, source_cells, target_cells, source_mass, target_mass, zeros)
    wide = lax.all_gather(wide, "t", tiled=True)
    col_pot = y_start
    for iteration in range(ITERS):
        row_parts = lax.all_to_all(row_part, "t", 0, 0)
        col_part, row_pot = call(
            col_kernel,
            (f32(Z, TB, BLOCK), f32(SB, BLOCK)),
            lists + [tall, flat, flat, flat, cols],
            "cols",
            [VMEM] + [VMEM] * 4,
        )(listed, gram, row_parts, source_log, col_pot)
        col_parts = lax.all_to_all(col_part, "z", 0, 0)
        near = ("x", "c") if iteration < ITERS - 1 else ("x", "c", "t")
        peers = XC if iteration < ITERS - 1 else XC * SB
        col_parts = call(merge_kernel, f32(peers, TB, BLOCK), [], "merge", [VMEM])(col_parts)
        col_parts = lax.all_to_all(col_parts, near, 0, 0)
        if iteration < ITERS - 1:
            row_part, col_pot = call(
                row_kernel,
                (f32(SB, SB, BLOCK), f32(TB, BLOCK)),
                lists + [flat, tall, tall, tall, rows],
                "rows",
                [VMEM] * 5,
            )(listed, gram, col_parts, target_mass, row_pot)
    row_pot, col_pot, mapped = call(
        map_kernel,
        (f32(SB, BLOCK), f32(TB, BLOCK), f32(SB * BLOCK, E)),
        [
            pltpu.SMEM((SB * TB + 1,), jnp.float32),
            sems(2 * SB + 1),
            pltpu.VMEM((SB - 1, HEIGHT, E), jnp.float32),
            pltpu.VMEM((TB * BLOCK, E), jnp.bfloat16),
            pltpu.VMEM((SB * BLOCK, TB * BLOCK), jnp.bfloat16),
            pltpu.VMEM((8, BLOCK), jnp.int32),
            pltpu.VMEM((SB, TB, BLOCK), jnp.float32),
            flat,
            tall,
            tall,
            tall,
            pltpu.VMEM((SB * BLOCK, E), jnp.float32),
            rows,
            cols,
        ],
        "mapping",
        [VMEM] * 8 + [ANY],
        out_specs=(ANY, ANY, ANY),
        limit=LIMIT,
    )(
        listed,
        col_parts,
        target_mass,
        row_pot,
        x_norm,
        y_start,
        source_cells,
        target_cells,
        wide,
    )
    return row_pot.reshape(-1), col_pot.reshape(-1), mapped


def solution(mesh):
    fine = Mesh(mesh.devices.reshape(Z, 4, 2, 4), ("z", "x", "c", "t"))
    return jax.shard_map(
        shards,
        mesh=fine,
        in_specs=(P(SRC, None), P("t", None), P(SRC), P("t"), P(SRC, "t", None), P(SRC, "t")),
        out_specs=(P(SRC), P("t"), P(SRC, None)),
        check_vma=False,
    )
```

```python
import jax
import jax.numpy as jnp
from jax import lax
from jax.experimental import pallas as pl
from jax.experimental.pallas import tpu as pltpu
from jax.sharding import Mesh
from jax.sharding import PartitionSpec as P

BLOCK = 128
ITERS = 3
SB = 4
TB = 16
MAXB = 32
E = 256
XC = 8
Z = 16
EPS = 0.02
SRC = ("z", "x", "c")


VMEM = pl.BlockSpec(memory_space=pltpu.VMEM)
ANY = pl.BlockSpec(memory_space=pl.ANY)
OFFSET = 70.0
FIRST = 5000000000
STEP = 4
BITS = 6
MIDDLE = 10.0
REACH = 74.0
FIRST_LIMIT = 52


def call(kernel, out_shape, scratch, name, specs, out_specs=None, flops=1000000):
    return pl.pallas_call(
        kernel,
        out_shape=out_shape,
        in_specs=specs,
        out_specs=out_specs or jax.tree.map(lambda unused: VMEM, out_shape),
        scratch_shapes=scratch,
        compiler_params=pltpu.CompilerParams(vmem_limit_bytes=16 * 1024 * 1024),
        cost_estimate=pl.CostEstimate(flops=flops, bytes_accessed=2000000, transcendentals=500000),
        name=name,
    )


def f32(*shape):
    return jax.ShapeDtypeStruct(shape, jnp.float32)


def fetch(listed, pairs):
    for k in range(MAXB // STEP):
        pairs[k] = listed[0, k]
    return listed[0, MAXB // STEP]


def packed(pairs_in, counts):
    lane = lax.broadcasted_iota(jnp.int32, (8, BLOCK), 1)
    words = jnp.where(lane == MAXB // STEP, counts[0, 0], 0)
    for k in range(MAXB // STEP):
        word = pairs_in[0, k * STEP]
        for j in range(1, STEP):
            word = word | (pairs_in[0, k * STEP + j] << (BITS * j))
        words = jnp.where(lane == k, word, words)
    return words


def each(live, body):
    whole = live >> 2

    def several(i, unused):
        body([(i, j) for j in range(STEP)])
        return unused

    def single(k, unused):
        body([(whole, k - whole * STEP)])
        return unused

    lax.fori_loop(0, whole, several, 0)
    lax.fori_loop(whole * STEP, live, single, 0)


def place(pairs, slot):
    value = pairs[slot[0]] >> (BITS * slot[1])
    return (value >> 4) & 3, value & 15


def entry(pairs, k):
    return place(pairs, (k >> 2, k & 3))


def turned(block):
    return jnp.transpose(block, (1, 0))


def log_sum(parts):
    top = jnp.max(parts, axis=0)
    return top + jnp.log(jnp.sum(jnp.exp(parts - top[None]), axis=0))


def in_range(logs):
    return jnp.max(jnp.abs(logs - MIDDLE)) <= REACH


def spread_rows(potential, spread):
    for p in range(SB):
        spread[p] = turned(jnp.broadcast_to(potential[p : p + 1], (BLOCK, BLOCK)))


def spread_cols(potential, spread):
    for q in range(TB):
        spread[q] = jnp.broadcast_to(potential[q : q + 1], (8, BLOCK))


def row_scores(gram, spread, p, q):
    score = spread[q][None] + gram[p, q].reshape(BLOCK // 8, 8, BLOCK)
    return score.reshape(BLOCK, BLOCK)


def row_totals(sums):
    return jnp.concatenate(
        [jnp.sum(turned(sums[p]), axis=0, keepdims=True) for p in range(SB)], axis=0
    )


def row_passes(pairs, live, gram, spread, peaks, sums, found, also):
    peaks[...] = jnp.full(peaks.shape, -jnp.inf, jnp.float32)
    sums[...] = jnp.zeros(sums.shape, jnp.float32)

    def first(k, unused):
        p, q = entry(pairs, k)
        peaks[p] = jnp.maximum(peaks[p], row_scores(gram, spread, p, q))
        return unused

    lax.fori_loop(0, live, first, 0)
    for p in range(SB):
        peaks[p] = jnp.broadcast_to(jnp.max(peaks[p], axis=1, keepdims=True), (BLOCK, BLOCK))

    def second(k, unused):
        p, q = entry(pairs, k)
        weight = jnp.exp(row_scores(gram, spread, p, q) - peaks[p])
        sums[p] += weight
        also(p, q, weight)
        return unused

    lax.fori_loop(0, live, second, 0)
    tops = jnp.concatenate([turned(peaks[p])[0:1] for p in range(SB)], axis=0)
    found[...] = tops + jnp.log(row_totals(sums))


def row_pass(pairs, live, gram, spread, before, row_spread, sums, found, peaks, also):
    sums[...] = jnp.zeros(sums.shape, jnp.float32)

    def only(slots):
        places = [place(pairs, slot) for slot in slots]
        weights = [jnp.exp(row_scores(gram, spread, p, q) + row_spread[p]) for p, q in places]
        for (p, q), weight in zip(places, weights):
            sums[p] += weight
            also(p, q, weight)

    each(live, only)
    logs = jnp.log(row_totals(sums))
    found[...] = logs - (before + OFFSET)

    @pl.when(jnp.logical_not(in_range(logs)))
    def again():
        row_passes(pairs, live, gram, spread, peaks, sums, found, also)


def folded(cells):
    wide = cells.astype(jnp.float32)
    square = wide * wide
    square = turned(square[:, :BLOCK] + square[:, BLOCK:])
    return jnp.sum(square, axis=0, keepdims=True) * (1.0 / (E * EPS))


def nothing(p, q, weight):
    return None


def zero_kernel(zeros):
    zeros[...] = jnp.zeros(zeros.shape, jnp.float32)


def gram_kernel(
    pairs_in,
    counts,
    x,
    y,
    mass,
    zeros,
    gram,
    partial,
    x_norm,
    y_start,
    log_mass,
    listed,
    pairs,
    spread,
    row_spread,
    peaks,
    sums,
    found,
):
    listed[...] = packed(pairs_in, counts)
    log_mass[...] = jnp.log(mass[...])
    for p in range(SB):
        x_norm[pl.ds(p, 1)] = folded(x[pl.ds(p * BLOCK, BLOCK), :])

    def chunk(c):
        cells = y[pl.ds(c * 2 * BLOCK, 2 * BLOCK), :]
        dims = (((1,), (1,)), ((), ()))
        crossed = lax.dot_general(x[...], cells, dims, preferred_element_type=jnp.float32)
        crossed = crossed * (2.0 / (E * EPS))
        for half in range(2):
            norm = folded(cells[half * BLOCK : (half + 1) * BLOCK])
            spread[2 * c + half] = jnp.broadcast_to(-norm, (8, BLOCK))
            for p in range(SB):
                gram[p, 2 * c + half] = crossed[
                    p * BLOCK : (p + 1) * BLOCK, half * BLOCK : (half + 1) * BLOCK
                ]

    for c in range(TB // 2):
        chunk(c)
    y_start[...] = spread[...][:, 0]
    before = zeros[...] - x_norm[...]
    spread_rows(before + OFFSET, row_spread)
    live = fetch(listed, pairs)
    row_pass(pairs, live, gram, spread, before, row_spread, sums, found, peaks, nothing)
    for d in range(SB):
        partial[d] = found[...]


def col_kernel(
    listed,
    gram,
    partials,
    mass_log,
    before,
    partial,
    potential,
    spread,
    pairs,
    col_spread,
    peaks,
    sums,
    found,
):
    potential[...] = mass_log[...] - log_sum(partials[...])
    spread_rows(potential[...] + OFFSET, spread)
    spread_cols(before[...], col_spread)
    sums[...] = jnp.zeros(sums.shape, jnp.float32)
    live = fetch(listed, pairs)

    def scores(p, q):
        return (spread[p] + gram[p, q]).reshape(BLOCK // 8, 8, BLOCK)

    def only(slots):
        places = [place(pairs, slot) for slot in slots]
        parts = [jnp.sum(jnp.exp(scores(p, q) + col_spread[q][None]), axis=0) for p, q in places]
        for (p, q), part in zip(places, parts):
            sums[q] += part

    each(live, only)
    logs = jnp.log(jnp.sum(sums[...], axis=1))
    found[...] = logs - (before[...] + OFFSET)

    @pl.when(jnp.logical_not(in_range(logs)))
    def again():
        peaks[...] = jnp.full(peaks.shape, -jnp.inf, jnp.float32)
        sums[...] = jnp.zeros(sums.shape, jnp.float32)

        def first(k, unused):
            p, q = entry(pairs, k)
            peaks[q] = jnp.maximum(peaks[q], jnp.max(scores(p, q), axis=0))
            return unused

        lax.fori_loop(0, live, first, 0)
        peaks[...] = jnp.broadcast_to(jnp.max(peaks[...], axis=1, keepdims=True), peaks.shape)

        def second(k, unused):
            p, q = entry(pairs, k)
            sums[q] += jnp.sum(jnp.exp(scores(p, q) - peaks[q][None]), axis=0)
            return unused

        lax.fori_loop(0, live, second, 0)
        found[...] = peaks[...][:, 0] - OFFSET + jnp.log(jnp.sum(sums[...], axis=1))

    for d in range(Z):
        partial[d] = found[...]


def merge_kernel(partials, merged):
    found = log_sum(partials[...])
    merged[...] = jnp.broadcast_to(found[None], merged.shape)


def row_kernel(
    listed,
    gram,
    partials,
    mass,
    before,
    row_spread,
    partial,
    potential,
    pairs,
    spread,
    peaks,
    sums,
    found,
):
    potential[...] = jnp.log(mass[...]) - log_sum(partials[...])
    spread_cols(potential[...], spread)
    live = fetch(listed, pairs)
    row_pass(
        pairs, live, gram, spread, before[...], row_spread, sums, found, peaks, nothing
    )
    for d in range(SB):
        partial[d] = found[...]


def map_kernel(
    listed,
    gram,
    partials,
    mass,
    before,
    row_spread,
    x_norm,
    y_start,
    y,
    packet,
    row_pot,
    col_pot,
    pairs,
    done,
    spread,
    peaks,
    sums,
    found,
    high,
    low,
    rows_out,
    cols_out,
):
    potential = jnp.log(mass[...]) - log_sum(partials[...])
    rows_out[...] = EPS * (before[...] + x_norm[...])
    cols_out[...] = EPS * (potential - y_start[...])
    copies = [
        pltpu.make_async_copy(rows_out, row_pot, done.at[0]),
        pltpu.make_async_copy(cols_out, col_pot, done.at[1]),
    ]
    for copy in copies:
        copy.start()
    spread_cols(potential, spread)
    high[...] = jnp.zeros(high.shape, jnp.bfloat16)
    low[...] = jnp.zeros(low.shape, jnp.bfloat16)

    def also(p, q, weight):
        rows = pl.ds(pl.multiple_of(p * BLOCK, BLOCK), BLOCK)
        cols = pl.ds(pl.multiple_of(q * BLOCK, BLOCK), BLOCK)
        leading = weight.astype(jnp.bfloat16)
        high[rows, cols] = leading
        low[rows, cols] = (weight - leading.astype(jnp.float32)).astype(jnp.bfloat16)

    live = fetch(listed, pairs)
    row_pass(pairs, live, gram, spread, before[...], row_spread, sums, found, peaks, also)
    total = jnp.dot(high[...], y[...], preferred_element_type=jnp.float32) + jnp.dot(
        low[...], y[...], preferred_element_type=jnp.float32
    )
    for p in range(SB):
        packet[p, pl.ds(0, BLOCK), :] = total[p * BLOCK : (p + 1) * BLOCK] / jnp.sum(
            sums[p], axis=1, keepdims=True
        )
        packet[p, pl.ds(BLOCK, 8), :] = jnp.concatenate(
            [jnp.broadcast_to(found[pl.ds(p, 1)], (8, BLOCK))] * 2, axis=1
        )
    for copy in copies:
        copy.wait()


def mix_kernel(packets, mapped):
    parts = jnp.concatenate([packets[t, pl.ds(BLOCK, 1), pl.ds(0, BLOCK)] for t in range(SB)])
    share = jnp.exp(parts - jnp.max(parts, axis=0, keepdims=True))
    share = share / jnp.sum(share, axis=0, keepdims=True)
    total = jnp.zeros((BLOCK, E), jnp.float32)
    for t in range(SB):
        factor = turned(jnp.broadcast_to(share[t : t + 1], (BLOCK, BLOCK)))
        total = total + jnp.concatenate([factor, factor], axis=1) * packets[t, pl.ds(0, BLOCK), :]
    mapped[...] = jnp.broadcast_to(total[None], mapped.shape)


def shards(source_cells, target_cells, source_mass, target_mass, pairs, counts):
    pairs = pairs.reshape(1, MAXB)
    counts = counts.reshape(1, 1)
    source_mass = source_mass.reshape(SB, BLOCK)
    target_mass = target_mass.reshape(TB, BLOCK)
    tall = pltpu.VMEM((SB, BLOCK, BLOCK), jnp.float32)
    flat = pltpu.VMEM((TB, 8, BLOCK), jnp.float32)
    rows = pltpu.VMEM((SB, BLOCK), jnp.float32)
    cols = pltpu.VMEM((TB, BLOCK), jnp.float32)
    dense = pltpu.VMEM((SB * BLOCK, TB * BLOCK), jnp.bfloat16)
    lists = [pltpu.SMEM((MAXB // STEP,), jnp.int32)]

    def sems(count):
        return pltpu.SemaphoreType.DMA((count,))

    zeros = call(zero_kernel, f32(SB, BLOCK), [], "zeros", [], flops=FIRST)()
    gram, row_part, x_norm, y_start, source_log, listed = call(
        gram_kernel,
        (
            f32(SB, TB, BLOCK, BLOCK),
            f32(SB, SB, BLOCK),
            f32(SB, BLOCK),
            f32(TB, BLOCK),
            f32(SB, BLOCK),
            jax.ShapeDtypeStruct((8, BLOCK), jnp.int32),
        ),
        lists + [flat, tall, tall, tall, rows],
        "gram",
        [VMEM] * 6,
    )(pairs, counts, source_cells, target_cells, source_mass, zeros)
    col_pot = y_start
    for iteration in range(ITERS):
        row_parts = lax.all_to_all(row_part, "t", 0, 0)
        col_part, row_pot, row_spread = call(
            col_kernel,
            (f32(Z, TB, BLOCK), f32(SB, BLOCK), f32(SB, BLOCK, BLOCK)),
            lists + [flat, flat, flat, cols],
            "cols",
            [VMEM] * 5,
        )(listed, gram, row_parts, source_log, col_pot)
        col_parts = lax.all_to_all(col_part, "z", 0, 0)
        col_parts = call(merge_kernel, f32(XC, TB, BLOCK), [], "merge", [VMEM])(col_parts)
        col_parts = lax.all_to_all(col_parts, ("x", "c"), 0, 0)
        if iteration < ITERS - 1:
            row_part, col_pot = call(
                row_kernel,
                (f32(SB, SB, BLOCK), f32(TB, BLOCK)),
                lists + [flat, tall, tall, rows],
                "rows",
                [VMEM] * 6,
            )(listed, gram, col_parts, target_mass, row_pot, row_spread)
    packet, row_pot, col_pot = call(
        map_kernel,
        (f32(SB, BLOCK + 8, E), f32(SB, BLOCK), f32(TB, BLOCK)),
        lists + [sems(2), flat, tall, tall, rows, dense, dense, rows, cols],
        "mapping",
        [VMEM] * 9,
        out_specs=(VMEM, ANY, ANY),
    )(listed, gram, col_parts, target_mass, row_pot, row_spread, x_norm, y_start, target_cells)
    packets = lax.all_to_all(packet, "t", 0, 0)
    quarters = call(mix_kernel, f32(SB, BLOCK, E), [], "mix", [VMEM])(packets)
    mapped = lax.all_to_all(quarters, "t", 0, 0)
    return row_pot.reshape(-1), col_pot.reshape(-1), mapped.reshape(SB * BLOCK, E)


def solution(mesh):
    fine = Mesh(mesh.devices.reshape(Z, 4, 2, 4), ("z", "x", "c", "t"))
    return jax.shard_map(
        shards,
        mesh=fine,
        in_specs=(P(SRC, None), P("t", None), P(SRC), P("t"), P(SRC, "t", None), P(SRC, "t")),
        out_specs=(P(SRC), P("t"), P(SRC, None)),
        check_vma=False,
    )
```

```python
import jax
import jax.numpy as jnp
from jax import lax
from jax.experimental import pallas as pl
from jax.experimental.pallas import tpu as pltpu
from jax.sharding import Mesh
from jax.sharding import PartitionSpec as P

BLOCK = 128
ITERS = 3
SB = 4
TB = 16
MAXB = 32
E = 256
XC = 8
Z = 16
EPS = 0.02
SRC = ("z", "x", "c")


VMEM = pl.BlockSpec(memory_space=pltpu.VMEM)
ANY = pl.BlockSpec(memory_space=pl.ANY)
OFFSET = 70.0
FIRST = 5000000000
STEP = 4
BITS = 6
MIDDLE = 10.0
REACH = 74.0
FIRST_LIMIT = 52


def call(kernel, out_shape, scratch, name, specs, out_specs=None, flops=1000000):
    return pl.pallas_call(
        kernel,
        out_shape=out_shape,
        in_specs=specs,
        out_specs=out_specs or jax.tree.map(lambda unused: VMEM, out_shape),
        scratch_shapes=scratch,
        compiler_params=pltpu.CompilerParams(vmem_limit_bytes=16 * 1024 * 1024),
        cost_estimate=pl.CostEstimate(flops=flops, bytes_accessed=2000000, transcendentals=500000),
        name=name,
    )


def f32(*shape):
    return jax.ShapeDtypeStruct(shape, jnp.float32)


def fetch(listed, pairs):
    for k in range(MAXB // STEP):
        pairs[k] = listed[0, k]
    return listed[0, MAXB // STEP]


def packed(pairs_in, counts):
    lane = lax.broadcasted_iota(jnp.int32, (8, BLOCK), 1)
    words = jnp.where(lane == MAXB // STEP, counts[0, 0], 0)
    for k in range(MAXB // STEP):
        word = pairs_in[0, k * STEP]
        for j in range(1, STEP):
            word = word | (pairs_in[0, k * STEP + j] << (BITS * j))
        words = jnp.where(lane == k, word, words)
    return words


def each(live, body):
    whole = live >> 2

    def several(i, unused):
        body([(i, j) for j in range(STEP)])
        return unused

    def single(k, unused):
        body([(whole, k - whole * STEP)])
        return unused

    lax.fori_loop(0, whole, several, 0)
    lax.fori_loop(whole * STEP, live, single, 0)


def place(pairs, slot):
    value = pairs[slot[0]] >> (BITS * slot[1])
    return (value >> 4) & 3, value & 15


def entry(pairs, k):
    return place(pairs, (k >> 2, k & 3))


def turned(block):
    return jnp.transpose(block, (1, 0))


def log_sum(parts):
    top = jnp.max(parts, axis=0)
    return top + jnp.log(jnp.sum(jnp.exp(parts - top[None]), axis=0))


def in_range(logs):
    return jnp.max(jnp.abs(logs - MIDDLE)) <= REACH


def spread_rows(potential, spread):
    for p in range(SB):
        spread[p] = turned(jnp.broadcast_to(potential[p : p + 1], (BLOCK, BLOCK)))


def spread_cols(potential, spread):
    for q in range(TB):
        spread[q] = jnp.broadcast_to(potential[q : q + 1], (8, BLOCK))


def row_scores(gram, spread, p, q):
    score = spread[q][None] + gram[p, q].reshape(BLOCK // 8, 8, BLOCK)
    return score.reshape(BLOCK, BLOCK)


def row_totals(sums):
    return jnp.concatenate(
        [jnp.sum(turned(sums[p]), axis=0, keepdims=True) for p in range(SB)], axis=0
    )


def row_passes(pairs, live, gram, spread, peaks, sums, found, also):
    peaks[...] = jnp.full(peaks.shape, -jnp.inf, jnp.float32)
    sums[...] = jnp.zeros(sums.shape, jnp.float32)

    def first(k, unused):
        p, q = entry(pairs, k)
        peaks[p] = jnp.maximum(peaks[p], row_scores(gram, spread, p, q))
        return unused

    lax.fori_loop(0, live, first, 0)
    for p in range(SB):
        peaks[p] = jnp.broadcast_to(jnp.max(peaks[p], axis=1, keepdims=True), (BLOCK, BLOCK))

    def second(k, unused):
        p, q = entry(pairs, k)
        weight = jnp.exp(row_scores(gram, spread, p, q) - peaks[p])
        sums[p] += weight
        also(p, q, weight)
        return unused

    lax.fori_loop(0, live, second, 0)
    tops = jnp.concatenate([turned(peaks[p])[0:1] for p in range(SB)], axis=0)
    found[...] = tops + jnp.log(row_totals(sums))


def row_pass(pairs, live, gram, spread, before, row_spread, sums, found, peaks, also):
    sums[...] = jnp.zeros(sums.shape, jnp.float32)

    def only(slots):
        places = [place(pairs, slot) for slot in slots]
        weights = [jnp.exp(row_scores(gram, spread, p, q) + row_spread[p]) for p, q in places]
        for (p, q), weight in zip(places, weights):
            sums[p] += weight
            also(p, q, weight)

    each(live, only)
    logs = jnp.log(row_totals(sums))
    found[...] = logs - (before + OFFSET)

    @pl.when(jnp.logical_not(in_range(logs)))
    def again():
        row_passes(pairs, live, gram, spread, peaks, sums, found, also)


def folded(cells):
    wide = cells.astype(jnp.float32)
    square = wide * wide
    square = turned(square[:, :BLOCK] + square[:, BLOCK:])
    return jnp.sum(square, axis=0, keepdims=True) * (1.0 / (E * EPS))


def nothing(p, q, weight):
    return None


def zero_kernel(zeros):
    zeros[...] = jnp.zeros(zeros.shape, jnp.float32)


def gram_kernel(
    pairs_in,
    counts,
    x,
    y,
    mass,
    zeros,
    gram,
    partial,
    x_norm,
    y_start,
    log_mass,
    listed,
    pairs,
    spread,
    row_spread,
    peaks,
    sums,
    found,
):
    listed[...] = packed(pairs_in, counts)
    log_mass[...] = jnp.log(mass[...])
    for p in range(SB):
        x_norm[pl.ds(p, 1)] = folded(x[pl.ds(p * BLOCK, BLOCK), :])

    def chunk(c):
        cells = y[pl.ds(c * 2 * BLOCK, 2 * BLOCK), :]
        dims = (((1,), (1,)), ((), ()))
        crossed = lax.dot_general(x[...], cells, dims, preferred_element_type=jnp.float32)
        crossed = crossed * (2.0 / (E * EPS))
        for half in range(2):
            norm = folded(cells[half * BLOCK : (half + 1) * BLOCK])
            spread[2 * c + half] = jnp.broadcast_to(-norm, (8, BLOCK))
            for p in range(SB):
                gram[p, 2 * c + half] = crossed[
                    p * BLOCK : (p + 1) * BLOCK, half * BLOCK : (half + 1) * BLOCK
                ]

    for c in range(TB // 2):
        chunk(c)
    y_start[...] = spread[...][:, 0]
    before = zeros[...] - x_norm[...]
    spread_rows(before + OFFSET, row_spread)
    live = fetch(listed, pairs)
    row_pass(pairs, live, gram, spread, before, row_spread, sums, found, peaks, nothing)
    for d in range(SB):
        partial[d] = found[...]


def col_kernel(
    listed,
    gram,
    partials,
    mass_log,
    before,
    partial,
    potential,
    spread,
    pairs,
    col_spread,
    peaks,
    sums,
    found,
):
    potential[...] = mass_log[...] - log_sum(partials[...])
    spread_rows(potential[...] + OFFSET, spread)
    spread_cols(before[...], col_spread)
    sums[...] = jnp.zeros(sums.shape, jnp.float32)
    live = fetch(listed, pairs)

    def scores(p, q):
        return (spread[p] + gram[p, q]).reshape(BLOCK // 8, 8, BLOCK)

    def only(slots):
        places = [place(pairs, slot) for slot in slots]
        parts = [jnp.sum(jnp.exp(scores(p, q) + col_spread[q][None]), axis=0) for p, q in places]
        for (p, q), part in zip(places, parts):
            sums[q] += part

    each(live, only)
    logs = jnp.log(jnp.sum(sums[...], axis=1))
    found[...] = logs - (before[...] + OFFSET)

    @pl.when(jnp.logical_not(in_range(logs)))
    def again():
        peaks[...] = jnp.full(peaks.shape, -jnp.inf, jnp.float32)
        sums[...] = jnp.zeros(sums.shape, jnp.float32)

        def first(k, unused):
            p, q = entry(pairs, k)
            peaks[q] = jnp.maximum(peaks[q], jnp.max(scores(p, q), axis=0))
            return unused

        lax.fori_loop(0, live, first, 0)
        peaks[...] = jnp.broadcast_to(jnp.max(peaks[...], axis=1, keepdims=True), peaks.shape)

        def second(k, unused):
            p, q = entry(pairs, k)
            sums[q] += jnp.sum(jnp.exp(scores(p, q) - peaks[q][None]), axis=0)
            return unused

        lax.fori_loop(0, live, second, 0)
        found[...] = peaks[...][:, 0] - OFFSET + jnp.log(jnp.sum(sums[...], axis=1))

    for d in range(partial.shape[0]):
        partial[d] = found[...]


def merge_kernel(partials, merged):
    found = log_sum(partials[...])
    merged[...] = jnp.broadcast_to(found[None], merged.shape)


def row_kernel(
    listed,
    gram,
    partials,
    mass,
    before,
    row_spread,
    partial,
    potential,
    pairs,
    spread,
    peaks,
    sums,
    found,
):
    potential[...] = jnp.log(mass[...]) - log_sum(partials[...])
    spread_cols(potential[...], spread)
    live = fetch(listed, pairs)
    row_pass(
        pairs, live, gram, spread, before[...], row_spread, sums, found, peaks, nothing
    )
    for d in range(SB):
        partial[d] = found[...]


def map_kernel(
    listed,
    gram,
    partials,
    mass,
    before,
    row_spread,
    x_norm,
    y_start,
    y,
    packet,
    row_pot,
    col_pot,
    pairs,
    done,
    spread,
    peaks,
    sums,
    found,
    high,
    low,
    rows_out,
    cols_out,
):
    potential = jnp.log(mass[...]) - log_sum(partials[...])
    rows_out[...] = EPS * (before[...] + x_norm[...])
    cols_out[...] = EPS * (potential - y_start[...])
    copies = [
        pltpu.make_async_copy(rows_out, row_pot, done.at[0]),
        pltpu.make_async_copy(cols_out, col_pot, done.at[1]),
    ]
    for copy in copies:
        copy.start()
    spread_cols(potential, spread)
    high[...] = jnp.zeros(high.shape, jnp.bfloat16)
    low[...] = jnp.zeros(low.shape, jnp.bfloat16)

    def also(p, q, weight):
        rows = pl.ds(pl.multiple_of(p * BLOCK, BLOCK), BLOCK)
        cols = pl.ds(pl.multiple_of(q * BLOCK, BLOCK), BLOCK)
        leading = weight.astype(jnp.bfloat16)
        high[rows, cols] = leading
        low[rows, cols] = (weight - leading.astype(jnp.float32)).astype(jnp.bfloat16)

    live = fetch(listed, pairs)
    row_pass(pairs, live, gram, spread, before[...], row_spread, sums, found, peaks, also)
    total = jnp.dot(high[...], y[...], preferred_element_type=jnp.float32) + jnp.dot(
        low[...], y[...], preferred_element_type=jnp.float32
    )
    for p in range(SB):
        packet[p, pl.ds(0, BLOCK), :] = total[p * BLOCK : (p + 1) * BLOCK] / jnp.sum(
            sums[p], axis=1, keepdims=True
        )
        packet[p, pl.ds(BLOCK, 8), :] = jnp.concatenate(
            [jnp.broadcast_to(found[pl.ds(p, 1)], (8, BLOCK))] * 2, axis=1
        )
    for copy in copies:
        copy.wait()


def mix_kernel(packets, mapped):
    parts = jnp.concatenate([packets[t, pl.ds(BLOCK, 1), pl.ds(0, BLOCK)] for t in range(SB)])
    share = jnp.exp(parts - jnp.max(parts, axis=0, keepdims=True))
    share = share / jnp.sum(share, axis=0, keepdims=True)
    total = jnp.zeros((BLOCK, E), jnp.float32)
    for t in range(SB):
        factor = turned(jnp.broadcast_to(share[t : t + 1], (BLOCK, BLOCK)))
        total = total + jnp.concatenate([factor, factor], axis=1) * packets[t, pl.ds(0, BLOCK), :]
    mapped[...] = jnp.broadcast_to(total[None], mapped.shape)


def shards(source_cells, target_cells, source_mass, target_mass, pairs, counts):
    pairs = pairs.reshape(1, MAXB)
    counts = counts.reshape(1, 1)
    source_mass = source_mass.reshape(SB, BLOCK)
    target_mass = target_mass.reshape(TB, BLOCK)
    tall = pltpu.VMEM((SB, BLOCK, BLOCK), jnp.float32)
    flat = pltpu.VMEM((TB, 8, BLOCK), jnp.float32)
    rows = pltpu.VMEM((SB, BLOCK), jnp.float32)
    cols = pltpu.VMEM((TB, BLOCK), jnp.float32)
    dense = pltpu.VMEM((SB * BLOCK, TB * BLOCK), jnp.bfloat16)
    lists = [pltpu.SMEM((MAXB // STEP,), jnp.int32)]

    def sems(count):
        return pltpu.SemaphoreType.DMA((count,))

    zeros = call(zero_kernel, f32(SB, BLOCK), [], "zeros", [], flops=FIRST)()
    gram, row_part, x_norm, y_start, source_log, listed = call(
        gram_kernel,
        (
            f32(SB, TB, BLOCK, BLOCK),
            f32(SB, SB, BLOCK),
            f32(SB, BLOCK),
            f32(TB, BLOCK),
            f32(SB, BLOCK),
            jax.ShapeDtypeStruct((8, BLOCK), jnp.int32),
        ),
        lists + [flat, tall, tall, tall, rows],
        "gram",
        [VMEM] * 6,
    )(pairs, counts, source_cells, target_cells, source_mass, zeros)
    col_pot = y_start
    for iteration in range(ITERS):
        far, near = ("z", Z), (("x", "c"), XC)
        first, second = (far, near) if iteration < ITERS - 1 else (near, far)
        row_parts = lax.all_to_all(row_part, "t", 0, 0)
        col_part, row_pot, row_spread = call(
            col_kernel,
            (f32(first[1], TB, BLOCK), f32(SB, BLOCK), f32(SB, BLOCK, BLOCK)),
            lists + [flat, flat, flat, cols],
            "cols",
            [VMEM] * 5,
        )(listed, gram, row_parts, source_log, col_pot)
        col_parts = lax.all_to_all(col_part, first[0], 0, 0)
        merged = f32(second[1], TB, BLOCK)
        col_parts = call(merge_kernel, merged, [], "merge", [VMEM])(col_parts)
        col_parts = lax.all_to_all(col_parts, second[0], 0, 0)
        if iteration < ITERS - 1:
            row_part, col_pot = call(
                row_kernel,
                (f32(SB, SB, BLOCK), f32(TB, BLOCK)),
                lists + [flat, tall, tall, rows],
                "rows",
                [VMEM] * 6,
            )(listed, gram, col_parts, target_mass, row_pot, row_spread)
    packet, row_pot, col_pot = call(
        map_kernel,
        (f32(SB, BLOCK + 8, E), f32(SB, BLOCK), f32(TB, BLOCK)),
        lists + [sems(2), flat, tall, tall, rows, dense, dense, rows, cols],
        "mapping",
        [VMEM] * 9,
        out_specs=(VMEM, ANY, ANY),
    )(listed, gram, col_parts, target_mass, row_pot, row_spread, x_norm, y_start, target_cells)
    packets = lax.all_to_all(packet, "t", 0, 0)
    quarters = call(mix_kernel, f32(SB, BLOCK, E), [], "mix", [VMEM])(packets)
    mapped = lax.all_to_all(quarters, "t", 0, 0)
    return row_pot.reshape(-1), col_pot.reshape(-1), mapped.reshape(SB * BLOCK, E)


def solution(mesh):
    fine = Mesh(mesh.devices.reshape(Z, 4, 2, 4), ("z", "x", "c", "t"))
    return jax.shard_map(
        shards,
        mesh=fine,
        in_specs=(P(SRC, None), P("t", None), P(SRC), P("t"), P(SRC, "t", None), P(SRC, "t")),
        out_specs=(P(SRC), P("t"), P(SRC, None)),
        check_vma=False,
    )
```

```python
import jax
import jax.numpy as jnp
from jax import lax
from jax.experimental import pallas as pl
from jax.experimental.pallas import tpu as pltpu
from jax.sharding import Mesh
from jax.sharding import PartitionSpec as P

BLOCK = 128
ITERS = 3
SB = 4
TB = 16
MAXB = 32
E = 256
XC = 8
Z = 16
EPS = 0.02
SRC = ("z", "x", "c")


VMEM = pl.BlockSpec(memory_space=pltpu.VMEM)
ANY = pl.BlockSpec(memory_space=pl.ANY)
OFFSET = 70.0
FIRST = 5000000000
STEP = 4
BITS = 6
MIDDLE = 10.0
REACH = 74.0
FIRST_LIMIT = 52


def call(kernel, out_shape, scratch, name, specs, out_specs=None, flops=1000000):
    return pl.pallas_call(
        kernel,
        out_shape=out_shape,
        in_specs=specs,
        out_specs=out_specs or jax.tree.map(lambda unused: VMEM, out_shape),
        scratch_shapes=scratch,
        compiler_params=pltpu.CompilerParams(vmem_limit_bytes=16 * 1024 * 1024),
        cost_estimate=pl.CostEstimate(flops=flops, bytes_accessed=2000000, transcendentals=500000),
        name=name,
    )


def f32(*shape):
    return jax.ShapeDtypeStruct(shape, jnp.float32)


def fetch(listed, pairs):
    for k in range(MAXB // STEP):
        pairs[k] = listed[0, k]
    return listed[0, MAXB // STEP]


def packed(pairs_in, counts):
    lane = lax.broadcasted_iota(jnp.int32, (8, BLOCK), 1)
    words = jnp.where(lane == MAXB // STEP, counts[0, 0], 0)
    for k in range(MAXB // STEP):
        word = pairs_in[0, k * STEP]
        for j in range(1, STEP):
            word = word | (pairs_in[0, k * STEP + j] << (BITS * j))
        words = jnp.where(lane == k, word, words)
    return words


def each(live, body):
    whole = live >> 2

    def several(i, unused):
        body([(i, j) for j in range(STEP)])
        return unused

    def single(k, unused):
        body([(whole, k - whole * STEP)])
        return unused

    lax.fori_loop(0, whole, several, 0)
    lax.fori_loop(whole * STEP, live, single, 0)


def place(pairs, slot):
    value = pairs[slot[0]] >> (BITS * slot[1])
    return (value >> 4) & 3, value & 15


def entry(pairs, k):
    return place(pairs, (k >> 2, k & 3))


def turned(block):
    return jnp.transpose(block, (1, 0))


def log_sum(parts):
    top = jnp.max(parts, axis=0)
    return top + jnp.log(jnp.sum(jnp.exp(parts - top[None]), axis=0))


def in_range(logs):
    return jnp.max(jnp.abs(logs - MIDDLE)) <= REACH


def spread_rows(potential, spread):
    for p in range(SB):
        spread[p] = turned(jnp.broadcast_to(potential[p : p + 1], (BLOCK, BLOCK)))


def spread_cols(potential, spread):
    for q in range(TB):
        spread[q] = jnp.broadcast_to(potential[q : q + 1], (8, BLOCK))


def row_scores(gram, spread, p, q):
    score = spread[q][None] + gram[p, q].reshape(BLOCK // 8, 8, BLOCK)
    return score.reshape(BLOCK, BLOCK)


def row_totals(sums):
    return jnp.concatenate(
        [jnp.sum(turned(sums[p]), axis=0, keepdims=True) for p in range(SB)], axis=0
    )


def row_passes(pairs, live, gram, spread, peaks, sums, found, also):
    peaks[...] = jnp.full(peaks.shape, -jnp.inf, jnp.float32)
    sums[...] = jnp.zeros(sums.shape, jnp.float32)

    def first(k, unused):
        p, q = entry(pairs, k)
        peaks[p] = jnp.maximum(peaks[p], row_scores(gram, spread, p, q))
        return unused

    lax.fori_loop(0, live, first, 0)
    for p in range(SB):
        peaks[p] = jnp.broadcast_to(jnp.max(peaks[p], axis=1, keepdims=True), (BLOCK, BLOCK))

    def second(k, unused):
        p, q = entry(pairs, k)
        weight = jnp.exp(row_scores(gram, spread, p, q) - peaks[p])
        sums[p] += weight
        also(p, q, weight)
        return unused

    lax.fori_loop(0, live, second, 0)
    tops = jnp.concatenate([turned(peaks[p])[0:1] for p in range(SB)], axis=0)
    found[...] = tops + jnp.log(row_totals(sums))


def row_pass(pairs, live, gram, spread, before, row_spread, sums, found, peaks, also):
    sums[...] = jnp.zeros(sums.shape, jnp.float32)

    def only(slots):
        places = [place(pairs, slot) for slot in slots]
        weights = [jnp.exp(row_scores(gram, spread, p, q) + row_spread[p]) for p, q in places]
        for (p, q), weight in zip(places, weights):
            sums[p] += weight
            also(p, q, weight)

    each(live, only)
    logs = jnp.log(row_totals(sums))
    found[...] = logs - (before + OFFSET)

    @pl.when(jnp.logical_not(in_range(logs)))
    def again():
        row_passes(pairs, live, gram, spread, peaks, sums, found, also)


def folded(cells):
    wide = cells.astype(jnp.float32)
    square = wide * wide
    square = turned(square[:, :BLOCK] + square[:, BLOCK:])
    return jnp.sum(square, axis=0, keepdims=True) * (1.0 / (E * EPS))


def nothing(p, q, weight):
    return None


def zero_kernel(zeros):
    zeros[...] = jnp.zeros(zeros.shape, jnp.float32)


def gram_kernel(
    pairs_in,
    counts,
    x,
    y,
    mass,
    zeros,
    gram,
    partial,
    x_norm,
    y_start,
    log_mass,
    listed,
    pairs,
    spread,
    row_spread,
    peaks,
    sums,
    found,
):
    listed[...] = packed(pairs_in, counts)
    log_mass[...] = jnp.log(mass[...])
    for p in range(SB):
        x_norm[pl.ds(p, 1)] = folded(x[pl.ds(p * BLOCK, BLOCK), :])

    def chunk(c):
        cells = y[pl.ds(c * 2 * BLOCK, 2 * BLOCK), :]
        dims = (((1,), (1,)), ((), ()))
        crossed = lax.dot_general(x[...], cells, dims, preferred_element_type=jnp.float32)
        crossed = crossed * (2.0 / (E * EPS))
        for half in range(2):
            norm = folded(cells[half * BLOCK : (half + 1) * BLOCK])
            spread[2 * c + half] = jnp.broadcast_to(-norm, (8, BLOCK))
            for p in range(SB):
                gram[p, 2 * c + half] = crossed[
                    p * BLOCK : (p + 1) * BLOCK, half * BLOCK : (half + 1) * BLOCK
                ]

    for c in range(TB // 2):
        chunk(c)
    y_start[...] = spread[...][:, 0]
    before = zeros[...] - x_norm[...]
    spread_rows(before + OFFSET, row_spread)
    live = fetch(listed, pairs)
    row_pass(pairs, live, gram, spread, before, row_spread, sums, found, peaks, nothing)
    for d in range(SB):
        partial[d] = found[...]


def col_kernel(
    listed,
    gram,
    partials,
    mass_log,
    before,
    partial,
    potential,
    spread,
    pairs,
    col_spread,
    peaks,
    sums,
    found,
):
    potential[...] = mass_log[...] - log_sum(partials[...])
    spread_rows(potential[...] + OFFSET, spread)
    spread_cols(before[...], col_spread)
    sums[...] = jnp.zeros(sums.shape, jnp.float32)
    live = fetch(listed, pairs)

    def scores(p, q):
        return (spread[p] + gram[p, q]).reshape(BLOCK // 8, 8, BLOCK)

    def only(slots):
        places = [place(pairs, slot) for slot in slots]
        parts = [jnp.sum(jnp.exp(scores(p, q) + col_spread[q][None]), axis=0) for p, q in places]
        for (p, q), part in zip(places, parts):
            sums[q] += part

    each(live, only)
    logs = jnp.log(jnp.sum(sums[...], axis=1))
    found[...] = logs - (before[...] + OFFSET)

    @pl.when(jnp.logical_not(in_range(logs)))
    def again():
        peaks[...] = jnp.full(peaks.shape, -jnp.inf, jnp.float32)
        sums[...] = jnp.zeros(sums.shape, jnp.float32)

        def first(k, unused):
            p, q = entry(pairs, k)
            peaks[q] = jnp.maximum(peaks[q], jnp.max(scores(p, q), axis=0))
            return unused

        lax.fori_loop(0, live, first, 0)
        peaks[...] = jnp.broadcast_to(jnp.max(peaks[...], axis=1, keepdims=True), peaks.shape)

        def second(k, unused):
            p, q = entry(pairs, k)
            sums[q] += jnp.sum(jnp.exp(scores(p, q) - peaks[q][None]), axis=0)
            return unused

        lax.fori_loop(0, live, second, 0)
        found[...] = peaks[...][:, 0] - OFFSET + jnp.log(jnp.sum(sums[...], axis=1))

    for d in range(partial.shape[0]):
        partial[d] = found[...]


def merge_kernel(partials, merged):
    found = log_sum(partials[...])
    merged[...] = jnp.broadcast_to(found[None], merged.shape)


def row_kernel(
    listed,
    gram,
    partials,
    mass,
    before,
    row_spread,
    partial,
    potential,
    pairs,
    spread,
    peaks,
    sums,
    found,
):
    potential[...] = jnp.log(mass[...]) - log_sum(partials[...])
    spread_cols(potential[...], spread)
    live = fetch(listed, pairs)
    row_pass(
        pairs, live, gram, spread, before[...], row_spread, sums, found, peaks, nothing
    )
    for d in range(SB):
        partial[d] = found[...]


def map_kernel(
    listed,
    gram,
    partials,
    mass,
    before,
    row_spread,
    x_norm,
    y_start,
    y,
    packet,
    row_pot,
    col_pot,
    pairs,
    done,
    spread,
    peaks,
    sums,
    found,
    high,
    low,
    rows_out,
    cols_out,
):
    potential = jnp.log(mass[...]) - log_sum(partials[...])
    rows_out[...] = EPS * (before[...] + x_norm[...])
    cols_out[...] = EPS * (potential - y_start[...])
    copies = [
        pltpu.make_async_copy(rows_out, row_pot, done.at[0]),
        pltpu.make_async_copy(cols_out, col_pot, done.at[1]),
    ]
    for copy in copies:
        copy.start()
    spread_cols(potential, spread)
    high[...] = jnp.zeros(high.shape, jnp.bfloat16)
    low[...] = jnp.zeros(low.shape, jnp.bfloat16)

    def also(p, q, weight):
        rows = pl.ds(pl.multiple_of(p * BLOCK, BLOCK), BLOCK)
        cols = pl.ds(pl.multiple_of(q * BLOCK, BLOCK), BLOCK)
        leading = weight.astype(jnp.bfloat16)
        high[rows, cols] = leading
        low[rows, cols] = (weight - leading.astype(jnp.float32)).astype(jnp.bfloat16)

    live = fetch(listed, pairs)
    row_pass(pairs, live, gram, spread, before[...], row_spread, sums, found, peaks, also)
    total = jnp.dot(high[...], y[...], preferred_element_type=jnp.float32) + jnp.dot(
        low[...], y[...], preferred_element_type=jnp.float32
    )
    for p in range(SB):
        packet[p, pl.ds(0, BLOCK), :] = total[p * BLOCK : (p + 1) * BLOCK] / jnp.sum(
            sums[p], axis=1, keepdims=True
        )
        packet[p, pl.ds(BLOCK, 8), :] = jnp.concatenate(
            [jnp.broadcast_to(found[pl.ds(p, 1)], (8, BLOCK))] * 2, axis=1
        )
    for copy in copies:
        copy.wait()


def mix_kernel(packets, mapped):
    parts = jnp.concatenate([packets[t, pl.ds(BLOCK, 1), pl.ds(0, BLOCK)] for t in range(SB)])
    share = jnp.exp(parts - jnp.max(parts, axis=0, keepdims=True))
    share = share / jnp.sum(share, axis=0, keepdims=True)
    total = jnp.zeros((BLOCK, E), jnp.float32)
    for t in range(SB):
        factor = turned(jnp.broadcast_to(share[t : t + 1], (BLOCK, BLOCK)))
        total = total + jnp.concatenate([factor, factor], axis=1) * packets[t, pl.ds(0, BLOCK), :]
    mapped[...] = jnp.broadcast_to(total[None], mapped.shape)


def shards(source_cells, target_cells, source_mass, target_mass, pairs, counts):
    pairs = pairs.reshape(1, MAXB)
    counts = counts.reshape(1, 1)
    source_mass = source_mass.reshape(SB, BLOCK)
    target_mass = target_mass.reshape(TB, BLOCK)
    tall = pltpu.VMEM((SB, BLOCK, BLOCK), jnp.float32)
    flat = pltpu.VMEM((TB, 8, BLOCK), jnp.float32)
    rows = pltpu.VMEM((SB, BLOCK), jnp.float32)
    cols = pltpu.VMEM((TB, BLOCK), jnp.float32)
    dense = pltpu.VMEM((SB * BLOCK, TB * BLOCK), jnp.bfloat16)
    lists = [pltpu.SMEM((MAXB // STEP,), jnp.int32)]

    def sems(count):
        return pltpu.SemaphoreType.DMA((count,))

    zeros = call(zero_kernel, f32(SB, BLOCK), [], "zeros", [], flops=FIRST)()
    gram, row_part, x_norm, y_start, source_log, listed = call(
        gram_kernel,
        (
            f32(SB, TB, BLOCK, BLOCK),
            f32(SB, SB, BLOCK),
            f32(SB, BLOCK),
            f32(TB, BLOCK),
            f32(SB, BLOCK),
            jax.ShapeDtypeStruct((8, BLOCK), jnp.int32),
        ),
        lists + [flat, tall, tall, tall, rows],
        "gram",
        [VMEM] * 6,
    )(pairs, counts, source_cells, target_cells, source_mass, zeros)
    col_pot = y_start
    for iteration in range(ITERS):
        far, near = ("z", Z), (("x", "c"), XC)
        first, second = (far, near) if 0 < iteration < ITERS - 1 else (near, far)
        row_parts = lax.all_to_all(row_part, "t", 0, 0)
        col_part, row_pot, row_spread = call(
            col_kernel,
            (f32(first[1], TB, BLOCK), f32(SB, BLOCK), f32(SB, BLOCK, BLOCK)),
            lists + [flat, flat, flat, cols],
            "cols",
            [VMEM] * 5,
        )(listed, gram, row_parts, source_log, col_pot)
        col_parts = lax.all_to_all(col_part, first[0], 0, 0)
        merged = f32(second[1], TB, BLOCK)
        col_parts = call(merge_kernel, merged, [], "merge", [VMEM])(col_parts)
        col_parts = lax.all_to_all(col_parts, second[0], 0, 0)
        if iteration < ITERS - 1:
            row_part, col_pot = call(
                row_kernel,
                (f32(SB, SB, BLOCK), f32(TB, BLOCK)),
                lists + [flat, tall, tall, rows],
                "rows",
                [VMEM] * 6,
            )(listed, gram, col_parts, target_mass, row_pot, row_spread)
    packet, row_pot, col_pot = call(
        map_kernel,
        (f32(SB, BLOCK + 8, E), f32(SB, BLOCK), f32(TB, BLOCK)),
        lists + [sems(2), flat, tall, tall, rows, dense, dense, rows, cols],
        "mapping",
        [VMEM] * 9,
        out_specs=(VMEM, ANY, ANY),
    )(listed, gram, col_parts, target_mass, row_pot, row_spread, x_norm, y_start, target_cells)
    packets = lax.all_to_all(packet, "t", 0, 0)
    quarters = call(mix_kernel, f32(SB, BLOCK, E), [], "mix", [VMEM])(packets)
    mapped = lax.all_to_all(quarters, "t", 0, 0)
    return row_pot.reshape(-1), col_pot.reshape(-1), mapped.reshape(SB * BLOCK, E)


def solution(mesh):
    fine = Mesh(mesh.devices.reshape(Z, 4, 2, 4), ("z", "x", "c", "t"))
    return jax.shard_map(
        shards,
        mesh=fine,
        in_specs=(P(SRC, None), P("t", None), P(SRC), P("t"), P(SRC, "t", None), P(SRC, "t")),
        out_specs=(P(SRC), P("t"), P(SRC, None)),
        check_vma=False,
    )
```
